512 devices in a mesh: crop: 2 (over y_lo), seq: 4 (over y_hi), res: 64 (over z, x, core).
Axes of the slice: x: 4, y: 8 (y_hi: 4, y_lo: 2; y = y_hi * 2 + y_lo), z: 8, core: 2. Of those that a mesh axis runs over, the one named last changes fastest.
Arguments:
- aligned_chain_embedding: bfloat16 [256, 256, 256], P(('crop', 'seq'), 'res'), parts along dimension 0, may hold values from -6 to 6
- alignment_mask: int32 [256, 256], P(('crop', 'seq'), 'res'), parts along dimension 0, may hold values from 0 to 1, as said below
- resolved_residue_mask: int32 [512], P('crop'), parts along dimension 0, may hold values 0 or 1
- pairwise_state: bfloat16 [512, 256, 128], P(('crop', 'seq'), 'res'), parts along dimension 0, may hold values from -8 to 8
- combined_projection_matrix: bfloat16 [256, 1024], replicated, may hold values from -0.375 to 0.375
- pair_bias_weight: bfloat16 [128, 8], replicated, may hold values from -8 to 8
- final_projection_matrix: bfloat16 [256, 256], replicated, may hold values from -0.375 to 0.375
- left_right_projection_matrix: bfloat16 [256, 64], replicated, may hold values from -1.5 to 1.5
- outer_mean_weight: bfloat16 [1024, 128], replicated, may hold values from -0.1875 to 0.1875
Outputs:
- alignment_output: bfloat16 [256, 256, 256], P(('crop', 'seq'), 'res'), parts along dimension 0
- pairwise_output: bfloat16 [512, 256, 128], P(('crop', 'seq'), 'res'), parts along dimension 0
The draws below stay inside these ranges and needn't reach their ends.
There are 2 independent parts, one for each index of `crop`. The reference program is written for one: setup_inputs(seed, part) draws one part's arguments, and reference() takes and returns one part's arrays. A program takes and returns all parts, laid end to end along the dimension named above; an argument that names none is the same for every part. Nothing has to cross between parts.
Inputs may be any that keep to these rules, and one draw needn't show every extreme that they name: `alignment_mask`: sequence 0 has no gaps.
All inputs are finite; a program needn't handle non-finite values.
Results may differ from the reference program's by a relative error of at most 0.013.
The reference program's roundings to bfloat16 on the way count: a program that leaves them out, or rounds other values in their place, can miss the bound.
Values may be sent and summed in bfloat16 or wider, within the bound.
No kernel may reach another device: no remote copies, remote signals or barrier semaphores. Data moves between devices by JAX's collectives and lax.ppermute only.
A program may use at most 64 MiB of HBM per device.

```python
import math
import jax
import jax.numpy as jnp
from jax import lax

ROW_FEATURES = 256
CZ = 128
HEAD_NUMBER = 8
PER_HEAD_DIM = 32
PROJ_FEATURES = 32
ALIGNED_CHAINS = 128
WINDOW_AMINOS = 256


def draw_alignment_mask(key, part):
    permutation_indices = jnp.arange(ALIGNED_CHAINS, dtype=jnp.int32)[:, None]
    uniform_bound = 900 - 600 * permutation_indices // max(ALIGNED_CHAINS - 1, 1)
    random_token = jax.random.randint(key, (ALIGNED_CHAINS, WINDOW_AMINOS), 0, 1000, dtype=jnp.int32)
    keep = jnp.logical_or(random_token < uniform_bound, permutation_indices == 0)
    return keep.astype(jnp.int32)


def draw_pairwise_state(key, part):
    noise_key = jax.random.fold_in(key, 0)
    noise = jax.random.normal(noise_key, (WINDOW_AMINOS, WINDOW_AMINOS, CZ), jnp.float32)
    return jnp.clip(noise, -8.0, 8.0).astype(jnp.bfloat16)


def draw_pair_bias_weight(key, part):
    base_key = jax.random.fold_in(key, 0)
    weights = jax.random.normal(base_key, (CZ, HEAD_NUMBER), jnp.float32) / math.sqrt(CZ)
    return jnp.clip(weights, -8.0, 8.0).astype(jnp.bfloat16)


def set_ends(values, own_key, low, high):
    longest = values.shape.index(max(values.shape))
    spots = []
    for shift in (0, 1):
        where = [jax.random.randint(jax.random.fold_in(own_key, axis), (), 0, length) for axis, length in enumerate(values.shape)]
        where[longest] = (where[longest] + shift) % values.shape[longest]
        spots.append(tuple(where))
    return values.at[spots[0]].set(low).at[spots[1]].set(high)


def block_scale(stream_key, extent, shards, least, largest):
    factor_of, own = 1.0, jax.random.fold_in(stream_key, 6)
    for position, blocks in shards:
        heights = jnp.exp(jax.random.uniform(jax.random.fold_in(own, position), (blocks,), jnp.float32, least / len(shards), largest / len(shards)))
        factor_of = factor_of * jnp.repeat(heights, extent[position] // blocks).reshape([-1 if axis == position else 1 for axis in range(len(extent))])
    return factor_of


def scatter_about(rng, shape, spread, bound, cuts=(), kind=jnp.bfloat16):
    level = block_scale(rng, shape, cuts, -0.22, 0.18) if cuts else 1.0
    values = jax.random.normal(rng, shape, jnp.float32) * spread * level
    return jnp.minimum(jnp.maximum(values, -bound), bound).astype(kind)


def setup_inputs(seed: int = 0, part: int = 0) -> dict:
    key_of = jax.random.split(jax.random.key(seed), 10)
    part_keys = jax.random.split(jax.random.fold_in(key_of[9], part), 10)
    return {
        "aligned_chain_embedding": scatter_about(part_keys[0], (ALIGNED_CHAINS, WINDOW_AMINOS, ROW_FEATURES), 1.0, 6.0, ((0, 4), (1, 64))),
        "alignment_mask": draw_alignment_mask(jax.random.fold_in(jax.random.fold_in(key_of[9], part), 71), part),
        "resolved_residue_mask": set_ends((jax.random.randint(part_keys[2], (WINDOW_AMINOS,), 0, 5) < 4).astype(jnp.int32), jax.random.fold_in(part_keys[2], 1), 0, 1),
        "pairwise_state": draw_pairwise_state(jax.random.fold_in(jax.random.fold_in(key_of[9], part), 71), part),
        "combined_projection_matrix": scatter_about(key_of[4], (ROW_FEATURES, 4 * ROW_FEATURES), ROW_FEATURES ** -0.5, 0.375),
        "pair_bias_weight": draw_pair_bias_weight(jax.random.fold_in(key_of[9], 71), part),
        "final_projection_matrix": scatter_about(key_of[6], (ROW_FEATURES, ROW_FEATURES), ROW_FEATURES ** -0.5, 0.375),
        "left_right_projection_matrix": scatter_about(key_of[7], (ROW_FEATURES, 2 * PROJ_FEATURES), (ROW_FEATURES // 16) ** -0.5, 1.5),
        "outer_mean_weight": scatter_about(key_of[8], (PROJ_FEATURES * PROJ_FEATURES, CZ), (PROJ_FEATURES * PROJ_FEATURES) ** -0.5, 0.1875),
    }


epsilon = 1e-05

def layer_normalize(values):
    values = values.astype(jnp.float32)
    average = lax.optimization_barrier(jnp.mean(values, axis=-1, keepdims=True))
    centered = values - average
    variance = lax.optimization_barrier(jnp.mean(centered * centered, axis=-1, keepdims=True))
    return centered * lax.rsqrt(variance + epsilon)

def reference(aligned_chain_embedding, alignment_mask, resolved_residue_mask, pairwise_state, combined_projection_matrix, pair_bias_weight, final_projection_matrix, left_right_projection_matrix, outer_mean_weight):
    standardized_rows = layer_normalize(aligned_chain_embedding).astype(jnp.bfloat16)
    linear_mapped = jnp.dot(standardized_rows.reshape(ALIGNED_CHAINS * WINDOW_AMINOS, ROW_FEATURES), combined_projection_matrix, preferred_element_type=jnp.float32)
    linear_mapped = linear_mapped.reshape(ALIGNED_CHAINS, WINDOW_AMINOS, 4, HEAD_NUMBER, PER_HEAD_DIM)
    queries = (linear_mapped[:, :, 0] * PER_HEAD_DIM ** (-0.5)).astype(jnp.bfloat16)
    key_rows = linear_mapped[:, :, 1].astype(jnp.bfloat16)
    value_rows = linear_mapped[:, :, 2].astype(jnp.bfloat16)
    sigmoid_factor = jax.nn.sigmoid(linear_mapped[:, :, 3])
    pair_normed = layer_normalize(pairwise_state).astype(jnp.bfloat16)
    head_bias = jnp.dot(pair_normed.reshape(WINDOW_AMINOS * WINDOW_AMINOS, CZ), pair_bias_weight, preferred_element_type=jnp.float32)
    head_bias = jnp.transpose(head_bias.astype(jnp.bfloat16).reshape(WINDOW_AMINOS, WINDOW_AMINOS, HEAD_NUMBER), (2, 0, 1)).astype(jnp.float32)
    key_validity_mask = (alignment_mask.astype(jnp.float32) - 1.0) * 1000000000.0

    def attend(inputs):
        query_one, key_one, value_one, mask_one = inputs
        scores = jnp.einsum('ihd,jhd->hij', query_one.astype(jnp.float32), key_one.astype(jnp.float32), precision=lax.Precision.HIGHEST)
        scores = scores + head_bias + mask_one[None, None, :]
        row_max = lax.optimization_barrier(jnp.max(scores, axis=-1, keepdims=True))
        exponent = jnp.exp(scores - row_max)
        weights = (exponent / lax.optimization_barrier(jnp.sum(exponent, axis=-1, keepdims=True))).astype(jnp.bfloat16)
        result = jnp.einsum('hij,jhd->ihd', weights.astype(jnp.float32), value_one.astype(jnp.float32), precision=lax.Precision.HIGHEST)
        return result.astype(jnp.bfloat16)
    softmax_mixed = lax.map(attend, (queries, key_rows, value_rows, key_validity_mask))
    sigmoid_scaled = (sigmoid_factor * softmax_mixed.astype(jnp.float32)).astype(jnp.bfloat16).reshape(ALIGNED_CHAINS * WINDOW_AMINOS, ROW_FEATURES)
    embedding_increment = jnp.dot(sigmoid_scaled, final_projection_matrix, preferred_element_type=jnp.float32).reshape(ALIGNED_CHAINS, WINDOW_AMINOS, ROW_FEATURES)
    alignment_output = (aligned_chain_embedding.astype(jnp.float32) + embedding_increment).astype(jnp.bfloat16)
    standardized_product = layer_normalize(alignment_output).astype(jnp.bfloat16)
    left_right_vectors = jnp.dot(standardized_product.reshape(ALIGNED_CHAINS * WINDOW_AMINOS, ROW_FEATURES), left_right_projection_matrix, preferred_element_type=jnp.float32).reshape(ALIGNED_CHAINS, WINDOW_AMINOS, 2, PROJ_FEATURES)
    entry_present = alignment_mask.astype(jnp.float32)[:, :, None]
    left_side = (left_right_vectors[:, :, 0] * entry_present).astype(jnp.bfloat16)
    right_side = (left_right_vectors[:, :, 1] * entry_present).astype(jnp.bfloat16)
    presence_mask_flags = alignment_mask.astype(jnp.bfloat16)
    counts = jnp.dot(presence_mask_flags.T, presence_mask_flags, preferred_element_type=jnp.float32)
    project = outer_mean_weight.astype(jnp.float32)
    block_rows = math.gcd(32, WINDOW_AMINOS)

    def outer_block(start):
        left_piece = lax.dynamic_slice_in_dim(left_side, start, block_rows, 1)
        product = jnp.einsum('sic,sje->ijce', left_piece.astype(jnp.float32), right_side.astype(jnp.float32), precision=lax.Precision.HIGHEST)
        flattened = product.reshape(block_rows * WINDOW_AMINOS, PROJ_FEATURES * PROJ_FEATURES)
        return jnp.dot(flattened, project, precision=lax.Precision.HIGHEST).reshape(block_rows, WINDOW_AMINOS, CZ)
    starts = jnp.arange(WINDOW_AMINOS // block_rows, dtype=jnp.int32) * block_rows
    outer = lax.map(outer_block, starts).reshape(WINDOW_AMINOS, WINDOW_AMINOS, CZ)
    pair_mask = (resolved_residue_mask[:, None] * resolved_residue_mask[None, :]).astype(jnp.float32)
    pairwise_output = (pairwise_state.astype(jnp.float32) + pair_mask[:, :, None] * (outer / counts[:, :, None])).astype(jnp.bfloat16)
    return (alignment_output, pairwise_output)
```

```python
import functools

import jax
import jax.numpy as jnp
from jax import lax
from jax.experimental import pallas as pl
from jax.experimental.pallas import tpu as pltpu
from jax.sharding import Mesh
from jax.sharding import PartitionSpec as P


F32 = jnp.float32
BF16 = jnp.bfloat16
HEADS, DIM = 8, 32
GROUPS, CHIPS, ROWS = 4, 32, 16
EPSILON = 1e-5
VMEM_LIMIT = 40 * 2**20


def iota(shape, dim):
    return lax.broadcasted_iota(jnp.int32, shape, dim)


def one_hot(condition):
    return jnp.where(condition, 1.0, 0.0).astype(BF16)


def dot(a, b):
    return jnp.dot(a, b, preferred_element_type=F32)


def dot_nt(a, b):
    return lax.dot_general(a, b, (((1,), (1,)), ((), ())), preferred_element_type=F32)


def dot_tn(a, b):
    return lax.dot_general(a, b, (((0,), (0,)), ((), ())), preferred_element_type=F32)


def standardized(*parts):
    count = sum(p.shape[-1] for p in parts)
    average = jnp.sum(sum(parts[1:], parts[0]), axis=-1, keepdims=True) * (1.0 / count)
    centered = [p - average for p in parts]
    squares = [d * d for d in centered]
    variance = jnp.sum(sum(squares[1:], squares[0]), axis=-1, keepdims=True) * (1.0 / count)
    scale = lax.rsqrt(variance + EPSILON)
    return [d * scale for d in centered]


def pack_kernel(x_ref, mask_ref, pair_ref, weight_ref, out_ref, message, pair_rows):
    (normed,) = standardized(pair_ref[...].astype(F32))
    for i in range(pair_ref.shape[0]):
        pair_rows[4 * i : 4 * i + 4, :] = normed[i]
    spread = one_hot(iota((HEADS, 128), 0) == (iota((HEADS, 128), 1) // 8) % 8)
    weight = dot(weight_ref[...], spread).astype(BF16)
    bias = dot(pair_rows[...].astype(BF16), weight)
    row, lane = iota((256, 128), 0), iota((256, 128), 1)
    own = (row // 32 == lane % 8) & ((row // 16) % 2 == lane // 64)
    bias = jnp.sum(jnp.where(own, bias, 0.0).reshape(16, 16, 128), axis=0)

    x = x_ref[...].astype(F32)
    message[:, 0:4, :] = x[:, :, :128]
    message[:, 8:12, :] = x[:, :, 128:]
    mask = mask_ref[...].astype(F32).astype(BF16)
    flat = message.reshape(CHIPS * ROWS, 128)
    for t in range(4):
        flat[pl.ds(12 + t, CHIPS, stride=ROWS), :] = dot(mask, one_hot(iota((4, 128), 0) == t))
    for g in range(GROUPS):
        message[:, 4:8, :] = jnp.broadcast_to(bias[4 * g : 4 * g + 4][None], (CHIPS, 4, 128))
        out_ref[g * CHIPS : (g + 1) * CHIPS] = message[...].astype(BF16)


def attend_kernel(place, own_ref, other_ref, weight_ref, final_ref, sides_ref, out_ref, message):
    g, _, c = place()
    low = iota((16, 8, 128), 1) < 4
    lane = iota((128, 128), 1)

    def first_halves(tiles):
        return jnp.where(low, tiles[:16], pltpu.roll(tiles[16:], 4, 1)).reshape(128, 128)

    def second_halves(tiles):
        return jnp.where(low, pltpu.roll(tiles[:16], 4, 1), tiles[16:]).reshape(128, 128)

    normed, raw, masks, biases = [], [], [], []
    for s in range(GROUPS):
        parts = []
        for ref in (own_ref, other_ref):
            tiles = ref[s * CHIPS : (s + 1) * CHIPS].astype(F32)
            x0, x1 = first_halves(tiles[:, :8]), first_halves(tiles[:, 8:])
            bias = second_halves(tiles[:, :8])
            present = second_halves(tiles[:, 8:])
            parts.append(
                (
                    jnp.concatenate(standardized(x0, x1), axis=1).astype(BF16),
                    jnp.concatenate([x0, x1], axis=1).astype(BF16),
                    present,
                    jnp.where(c == 0, bias, pltpu.roll(bias, 64, 1)),
                )
            )
        normed.append([p[0] for p in parts])
        raw.append(parts[0][1])
        masks.append([p[2] for p in parts])
        biases.append([p[3] for p in parts])

    def rows_of(values):
        return jnp.concatenate([v.T for v in values], axis=1)

    pair_bias = jnp.concatenate(
        [
            rows_of(
                [
                    jnp.where(lane < 64, biases[2 * n][o], pltpu.roll(biases[2 * n + 1][o], 64, 1))
                    for o in range(2)
                ]
            )
            for n in range(2)
        ],
        axis=0,
    )
    mask_rows = rows_of(
        [
            jnp.where(
                lane < 64,
                jnp.where(lane < 32, masks[0][o], masks[1][o]),
                jnp.where(lane < 96, masks[2][o], masks[3][o]),
            )
            for o in range(2)
        ]
    )

    query, key = iota((CHIPS, 128), 0), iota((CHIPS, 128), 1)
    select = one_hot(key == (query % 16) * 8 + (query // 16) * 4 + g)
    of_head = jnp.where(
        iota((HEADS, 8, 256), 2) // DIM == iota((HEADS, 8, 256), 0), 1.0, 0.0
    )
    gated, residual, present = [], [], []
    for s in range(GROUPS):
        all_normed = jnp.concatenate(normed[s], axis=0)
        key_value = dot(all_normed, weight_ref[:, 256:768]).astype(BF16)
        mine = dot(select, normed[s][0]).astype(BF16)
        residual.append(dot(select, raw[s]))
        present.append(dot(select, masks[s][0].astype(BF16)))
        queries = (dot(mine, weight_ref[:, :256]) * DIM**-0.5).astype(BF16).astype(F32)
        gate = jax.nn.sigmoid(dot(mine, weight_ref[:, 768:]))
        spread = queries.reshape(GROUPS, 1, 8, 256) * of_head[None]
        scores = dot_nt(spread.reshape(256, 256).astype(BF16), key_value[:, :256])
        scores = scores + pair_bias + (mask_rows[32 * s : 32 * s + 1] - 1.0) * 1e9
        exponent = jnp.exp(scores - jnp.max(scores, axis=-1, keepdims=True))
        weights = (exponent / jnp.sum(exponent, axis=-1, keepdims=True)).astype(BF16)
        mixed = dot(weights, key_value[:, 256:]).reshape(GROUPS, HEADS, 8, 256) * of_head[None]
        attended = jnp.sum(mixed, axis=1).reshape(CHIPS, 256).astype(BF16)
        gated.append((gate * attended.astype(F32)).astype(BF16))
    gated = jnp.concatenate(gated, axis=0)
    residual = jnp.concatenate(residual, axis=0)
    present = jnp.concatenate(present, axis=0)

    result = (residual + dot(gated, final_ref[...])).astype(BF16).astype(F32)
    (normed_out,) = standardized(result)
    entry, place_of = iota((64, 256), 0), iota((64, 256), 1)
    four_times = one_hot(entry == (place_of // 128) * 32 + place_of % 32)
    sides = dot(normed_out.astype(BF16), dot(sides_ref[...], four_times).astype(BF16))
    left = (sides[:, :128] * present).astype(BF16)
    right = (sides[:, 128:] * present).astype(BF16).astype(F32)

    new, old = iota((128, 128), 0), iota((128, 128), 1)
    moved = one_hot(
        old == ((new // 2) % 4) * 32 + ((new // 8) % 4) * 8 + (new % 2) * 4 + new // 32
    )
    left = jnp.where(lane // 32 == new // 32, dot(moved, left), 0.0)
    left = jnp.sum(left.reshape(4, 32, 128), axis=0)
    left_mask = jnp.where(lane == 64 + g * 8 + new % 8, present, 0.0).astype(BF16)
    to, of = iota((16, 128), 0), iota((16, 128), 1)
    left_mask = dot(one_hot((of // 32 == to % 4) & ((of // 8) % 4 == to // 4)), left_mask)
    right = jnp.where(lane < 32, right, jnp.where(lane < 64, present, 0.0))

    flat = message.reshape(CHIPS * ROWS, 128)
    message[:, 8:16, :] = jnp.zeros((CHIPS, 8, 128), F32)
    for n in range(GROUPS):
        message[:, 0:8, :] = jnp.broadcast_to(left[8 * n : 8 * n + 8][None], (CHIPS, 8, 128))
        for s in range(GROUPS):
            flat[pl.ds(8 + s, CHIPS, stride=ROWS), :] = (
                right[s * CHIPS : (s + 1) * CHIPS] + left_mask[4 * n + s : 4 * n + s + 1]
            )
        for half in range(2):
            flat[pl.ds(12 + half, CHIPS, stride=ROWS), :] = result[
                n * CHIPS : (n + 1) * CHIPS, half * 128 : (half + 1) * 128
            ]
        out_ref[n * CHIPS : (n + 1) * CHIPS] = message[...].astype(BF16)


def outer_kernel(
    place, own_ref, other_ref, pair_ref, resolved_ref, weight_ref, align_ref, out_ref, own, other, align, product, update
):
    g, k, c = place()
    own[...] = own_ref[...].astype(F32).reshape(own.shape)
    other[...] = other_ref[...].astype(F32).reshape(other.shape)
    lane = iota((128, 128), 1)

    def row_of(ref, source, row):
        return ref[pl.ds(source * CHIPS * ROWS + row, CHIPS, stride=ROWS), :]

    def by_sequence(ref, source, first, step):
        return jnp.concatenate([row_of(ref, source, first + step * s) for s in range(GROUPS)], axis=0)

    for t in range(GROUPS):
        for half in range(2):
            align[pl.ds(half * 128 + t, CHIPS, stride=4), :] = row_of(own, t, 12 + half)
    for s in range(CHIPS):
        for half in range(2):
            rows = align[half * 128 + 4 * s : half * 128 + 4 * s + 4, :]
            align_ref[s, :, half * 128 : (half + 1) * 128] = rows.astype(BF16)

    right = jnp.zeros((128, 128), F32)
    right_mask = jnp.zeros((128, 128), F32)
    own_mask = jnp.zeros((128, 128), F32)
    other_mask = jnp.zeros((128, 128), F32)
    for t in range(GROUPS):
        mine = by_sequence(own, t, 8, 1)
        here = lane // 32 == t
        right = jnp.where(here, pltpu.roll(mine, 32 * t, 1), right)
        right_mask = jnp.where(here, pltpu.roll(mine, (32 * t + 96) % 128, 1), right_mask)
        own_mask = own_mask + mine
        other_mask = other_mask + by_sequence(other, t, 8, 1)
    left_mask = jnp.where(
        lane < 32, pltpu.roll(own_mask, 64, 1), jnp.where(lane < 64, pltpu.roll(other_mask, 96, 1), 0.0)
    )
    counts = dot_tn(left_mask.astype(BF16), right_mask.astype(BF16))

    right = right.astype(BF16)
    for o, ref in enumerate((own, other)):
        for t in range(GROUPS):
            for half in range(2):
                slab = (o * GROUPS + t) * 2 + half
                left = by_sequence(ref, t, half, 2).astype(BF16)
                product[slab * 128 : (slab + 1) * 128, :] = dot_tn(left, right)

    wide = iota((64, 128), 1) // 32
    total = jnp.zeros((256, 128), F32)
    for n in range(8):
        given = [product[pl.ds(4 * n + m, 64, stride=32), :] for m in range(4)]
        turned = []
        for j in range(4):
            tile = given[j]
            for m in range(4):
                if m != j:
                    tile = jnp.where(wide == m, pltpu.roll(given[m], (32 * (m - j)) % 128, 1), tile)
            turned.append(tile.astype(BF16))
        total = total + dot(jnp.concatenate(turned, axis=0), weight_ref[n * 128 : (n + 1) * 128, :])

    for o in range(2):
        core = c if o == 0 else 1 - c
        for t in range(GROUPS):
            first = (o * GROUPS + t) * 8
            for j in range(4):
                value = total[j * 64 + first : j * 64 + first + 8] / counts[first : first + 8, 32 * j : 32 * j + 1]
                update[pl.ds((4 * core + t) * 4 + j, 8, stride=32), :] = value

    row, column = iota((256, 256), 0), iota((256, 256), 1)
    resolved = jnp.broadcast_to(resolved_ref[...].astype(F32), (128, 256)).astype(BF16)
    row_mask = dot_nt(one_hot(column == 64 * g + row // 4), resolved)
    column_mask = dot_nt(one_hot(column == 8 * k + 4 * c + row % 4), resolved)
    update[...] = row_mask * column_mask * update[...]
    for i in range(64):
        out_ref[i] = (pair_ref[i].astype(F32) + update[4 * i : 4 * i + 4, :]).astype(BF16)


def call(kernel, shapes, scratch, flops, size, interpret=False):
    return pl.pallas_call(
        kernel,
        out_shape=shapes,
        scratch_shapes=scratch,
        compiler_params=pltpu.CompilerParams(vmem_limit_bytes=VMEM_LIMIT),
        cost_estimate=pl.CostEstimate(flops=flops, bytes_accessed=size, transcendentals=0),
        interpret=interpret,
    )


MESSAGES = jax.ShapeDtypeStruct((GROUPS * CHIPS, ROWS, 128), BF16)


def pack(x, mask, pair, weight, interpret=False):
    scratch = [pltpu.VMEM((CHIPS, ROWS, 128), F32), pltpu.VMEM((256, 128), F32)]
    return call(pack_kernel, MESSAGES, scratch, 10**7, 10**6, interpret)(x, mask, pair, weight)


def attend(place, own, other, weight, final, sides, interpret=False):
    scratch = [pltpu.VMEM((CHIPS, ROWS, 128), F32)]
    return call(functools.partial(attend_kernel, place), MESSAGES, scratch, 10**9, 2 * 10**6, interpret)(
        own, other, weight, final, sides
    )


def outer(place, own, other, pair, resolved, weight, interpret=False):
    scratch = [
        pltpu.VMEM((GROUPS * CHIPS * ROWS, 128), F32),
        pltpu.VMEM((GROUPS * CHIPS * ROWS, 128), F32),
        pltpu.VMEM((256, 128), F32),
        pltpu.VMEM((2048, 128), F32),
        pltpu.VMEM((256, 128), F32),
    ]
    shapes = (jax.ShapeDtypeStruct((CHIPS, 4, 256), BF16), jax.ShapeDtypeStruct((64, 4, 128), BF16))
    return call(functools.partial(outer_kernel, place), shapes, scratch, 10**9, 2 * 10**6, interpret)(
        own, other, pair, resolved.reshape(1, 256), weight
    )


def my_place():
    return lax.axis_index("seq"), lax.axis_index("chip"), lax.axis_index("core")


def exchange(messages):
    return lax.all_to_all(messages, ("seq", "chip"), 0, 0, tiled=True)


def from_other_core(x):
    return lax.ppermute(x, "core", [(0, 1), (1, 0)])


def per_device(x, mask, resolved, pair, combined, bias_weight, final, sides, outer_weight):
    own = exchange(pack(x, mask, pair, bias_weight))
    second = attend(my_place, own, from_other_core(own), combined, final, sides)
    own = exchange(second)
    return outer(my_place, own, from_other_core(own), pair, resolved, outer_weight)


def solution(mesh):
    crop, seq, res = (mesh.shape[a] for a in ("crop", "seq", "res"))
    fine = Mesh(mesh.devices.reshape(crop, seq, res // 2, 2), ("crop", "seq", "chip", "core"))
    rows, columns = ("crop", "seq"), ("chip", "core")
    placed = (P(rows, columns, None), P(rows, columns), P("crop"), P(rows, columns, None)) + (P(),) * 5
    return jax.shard_map(
        per_device,
        mesh=fine,
        in_specs=placed,
        out_specs=(P(rows, columns, None), P(rows, columns, None)),
        check_vma=False,
    )
```

```python
import functools

import jax
import jax.numpy as jnp
from jax import lax
from jax.experimental import pallas as pl
from jax.experimental.pallas import tpu as pltpu
from jax.sharding import Mesh
from jax.sharding import PartitionSpec as P


F32 = jnp.float32
BF16 = jnp.bfloat16
HEADS, DIM = 8, 32
GROUPS, CHIPS, ROWS = 4, 32, 16
SENT = GROUPS * CHIPS
EPSILON = 1e-5
VMEM_LIMIT = 40 * 2**20


def iota(shape, dim):
    return lax.broadcasted_iota(jnp.int32, shape, dim)


def one_hot(condition):
    return jnp.where(condition, 1.0, 0.0).astype(BF16)


def dot(a, b):
    return jnp.dot(a, b, preferred_element_type=F32)


def dot_nt(a, b):
    return lax.dot_general(a, b, (((1,), (1,)), ((), ())), preferred_element_type=F32)


def dot_tn(a, b):
    return lax.dot_general(a, b, (((0,), (0,)), ((), ())), preferred_element_type=F32)


def standardized(*parts):
    count = sum(p.shape[-1] for p in parts)
    average = jnp.sum(sum(parts[1:], parts[0]), axis=-1, keepdims=True) * (1.0 / count)
    centered = [p - average for p in parts]
    squares = [d * d for d in centered]
    variance = jnp.sum(sum(squares[1:], squares[0]), axis=-1, keepdims=True) * (1.0 / count)
    scale = lax.rsqrt(variance + EPSILON)
    return [d * scale for d in centered]


def pack_kernel(x_hbm, mask_hbm, pair_hbm, weight_hbm, out_ref, x_ref, mask_ref, pair_ref, weight_ref, message, pair_rows, arrived):
    copies = [
        pltpu.make_async_copy(source, to, arrived.at[n])
        for n, (source, to) in enumerate(
            [(pair_hbm, pair_ref), (x_hbm, x_ref), (weight_hbm, weight_ref), (mask_hbm, mask_ref)]
        )
    ]
    for copy in copies:
        copy.start()
    for copy in copies:
        copy.wait()
    (normed,) = standardized(pair_ref[...].astype(F32))
    for i in range(pair_ref.shape[0]):
        pair_rows[4 * i : 4 * i + 4, :] = normed[i]
    spread = one_hot(iota((HEADS, 128), 0) == (iota((HEADS, 128), 1) // 8) % 8)
    weight = dot_tn(weight_ref[...], spread).astype(BF16)
    bias = dot(pair_rows[...].astype(BF16), weight)
    row, lane = iota((256, 128), 0), iota((256, 128), 1)
    own = (row // 32 == lane % 8) & ((row // 16) % 2 == lane // 64)
    bias = jnp.sum(jnp.where(own, bias, 0.0).reshape(16, 16, 128), axis=0)

    x = x_ref[...].astype(F32)
    message[:, 0:4, :] = x[:, :, :128]
    message[:, 8:12, :] = x[:, :, 128:]
    mask = mask_ref[...].astype(F32).astype(BF16)
    flat = message.reshape(CHIPS * ROWS, 128)
    flat[pl.ds(12, CHIPS, stride=ROWS), :] = dot_tn(mask, one_hot(iota((4, 128), 0) == iota((4, 128), 1) // 32))
    for g in range(GROUPS):
        message[:, 4:8, :] = jnp.broadcast_to(bias[4 * g : 4 * g + 4][None], (CHIPS, 4, 128))
        out_ref[g * CHIPS : (g + 1) * CHIPS] = message[:, 0:13, :].astype(BF16)


def attend_kernel(place, own_ref, other_ref, weight_ref, final_ref, sides_ref, out_ref, wide, message):
    g, _, c = place()
    low = iota((16, 8, 128), 1) < 4
    lane = iota((128, 128), 1)

    def first_halves(tiles):
        return jnp.where(low, tiles[:16], pltpu.roll(tiles[16:], 4, 1)).reshape(128, 128)

    def second_halves(tiles):
        return jnp.where(low, pltpu.roll(tiles[:16], 4, 1), tiles[16:]).reshape(128, 128)

    normed, raw, masks, biases = [], [], [], []
    flat = wide.reshape(2 * SENT * ROWS, 128)
    for s in range(GROUPS):
        parts = []
        for o, ref in enumerate((own_ref, other_ref)):
            first = o * SENT + s * CHIPS
            wide[first : first + CHIPS, 0:13, :] = ref[s * CHIPS : (s + 1) * CHIPS].astype(F32)
            tiles = wide[first : first + CHIPS, 0:8, :]
            x0, x1 = first_halves(tiles), first_halves(wide[first : first + CHIPS, 8:16, :])
            bias = second_halves(tiles)
            parts.append(
                (
                    jnp.concatenate(standardized(x0, x1), axis=1).astype(BF16),
                    jnp.concatenate([x0, x1], axis=1).astype(BF16),
                    flat[pl.ds(first * ROWS + 12, CHIPS, stride=ROWS), :].astype(BF16),
                    jnp.where(c == 0, bias, pltpu.roll(bias, 64, 1)),
                )
            )
        normed.append(jnp.concatenate([p[0] for p in parts], axis=0))
        raw.append(jnp.concatenate([p[1] for p in parts], axis=0))
        masks.append([p[2] for p in parts])
        biases.append([p[3] for p in parts])

    def rows_of(values):
        return jnp.concatenate([v.T for v in values], axis=1)

    pair_bias = jnp.concatenate(
        [
            rows_of(
                [
                    jnp.where(lane < 64, biases[2 * n][o], pltpu.roll(biases[2 * n + 1][o], 64, 1))
                    for o in range(2)
                ]
            )
            for n in range(2)
        ],
        axis=0,
    )
    all_masks = jnp.concatenate([m for pair in masks for m in pair], axis=0)
    all_masks = dot(all_masks, one_hot(iota((128, 128), 0) == 32 * (lane % 4))).reshape(8, CHIPS, 128)
    chip, key = iota((8, CHIPS, 128), 1), iota((8, CHIPS, 128), 2)
    mask_rows = jnp.sum(jnp.where(chip == key // 8 + 16 * ((key // 4) % 2), all_masks, 0.0), axis=1)

    query, key = iota((CHIPS, 256), 0), iota((CHIPS, 256), 1)
    select = one_hot(key == (query % 16) * 8 + (query // 16) * 4 + g)
    my_mask = one_hot(iota((128, 128), 0) == 32 * g)
    of_head = jnp.where(
        iota((HEADS, 8, 256), 2) // DIM == iota((HEADS, 8, 256), 0), 1.0, 0.0
    )
    gated, residual, present = [], [], []
    for s in range(GROUPS):
        key_value = dot(normed[s], weight_ref[:, 256:768]).astype(BF16)
        mine = dot(select, normed[s]).astype(BF16)
        residual.append(dot(select, raw[s]))
        present.append(dot(masks[s][0], my_mask))
        queries = (dot(mine, weight_ref[:, :256]) * DIM**-0.5).astype(BF16).astype(F32)
        gate = jax.nn.sigmoid(dot(mine, weight_ref[:, 768:]))
        spread = queries.reshape(GROUPS, 1, 8, 256) * of_head[None]
        scores = dot_nt(spread.reshape(256, 256).astype(BF16), key_value[:, :256])
        key_mask = jnp.concatenate([mask_rows[2 * s : 2 * s + 1], mask_rows[2 * s + 1 : 2 * s + 2]], axis=1)
        scores = scores + pair_bias + (key_mask - 1.0) * 1e9
        exponent = jnp.exp(scores - jnp.max(scores, axis=-1, keepdims=True))
        weights = (exponent / jnp.sum(exponent, axis=-1, keepdims=True)).astype(BF16)
        mixed = dot(weights, key_value[:, 256:]).reshape(GROUPS, HEADS, 8, 256) * of_head[None]
        attended = jnp.sum(mixed, axis=1).reshape(CHIPS, 256).astype(BF16)
        gated.append((gate * attended.astype(F32)).astype(BF16))
    gated = jnp.concatenate(gated, axis=0)
    residual = jnp.concatenate(residual, axis=0)
    present = jnp.concatenate(present, axis=0)

    result = (residual + dot(gated, final_ref[...])).astype(BF16).astype(F32)
    (normed_out,) = standardized(result)
    entry, place_of = iota((64, 256), 0), iota((64, 256), 1)
    four_times = one_hot(entry == (place_of // 128) * 32 + place_of % 32)
    sides = dot(normed_out.astype(BF16), dot_tn(sides_ref[...], four_times).astype(BF16))
    left = (sides[:, :128] * present).astype(BF16)
    right = (sides[:, 128:] * present).astype(BF16).astype(F32)

    new, old = iota((128, 128), 0), iota((128, 128), 1)
    moved = one_hot(
        old == ((new // 2) % 4) * 32 + ((new // 8) % 4) * 8 + (new % 2) * 4 + new // 32
    )
    left = jnp.where(lane // 32 == new // 32, dot(moved, left), 0.0)
    left = jnp.sum(left.reshape(4, 32, 128), axis=0)
    row = new
    left_mask = jnp.where(lane == 32 * (row // 32) + 8 * g + row % 8, present, 0.0).astype(BF16)
    left_mask = dot(one_hot((iota((8, 128), 1) // 8) % 4 == iota((8, 128), 0)), left_mask)
    sequence = iota((CHIPS, 128), 1) // 32
    right_at = (iota((CHIPS, 128), 1) // 8) % 4 == (g + 1) % 4
    right_row, mask_row = jnp.zeros((CHIPS, 128), F32), jnp.zeros((CHIPS, 128), F32)
    for s in range(GROUPS):
        mine = slice(s * CHIPS, (s + 1) * CHIPS)
        right_row = jnp.where(sequence == s, right[mine], right_row)
        mask_row = jnp.where((sequence == s) & right_at, present[mine], mask_row)

    flat = message.reshape(CHIPS * ROWS, 128)
    flat[pl.ds(8, CHIPS, stride=ROWS), :] = right_row
    for n in range(GROUPS):
        message[:, 0:8, :] = jnp.broadcast_to(left[8 * n : 8 * n + 8][None], (CHIPS, 8, 128))
        flat[pl.ds(9, CHIPS, stride=ROWS), :] = mask_row + left_mask[n : n + 1]
        for half in range(2):
            flat[pl.ds(10 + half, CHIPS, stride=ROWS), :] = result[
                n * CHIPS : (n + 1) * CHIPS, half * 128 : (half + 1) * 128
            ]
        for part in range(3):
            out_ref[n * CHIPS : (n + 1) * CHIPS, part] = message[:, 4 * part : 4 * part + 4, :].astype(BF16)


def outer_kernel(place, both_ref, pair_ref, resolved_ref, weight_ref, align_ref, out_ref, wide, align, product, update):
    g, k, c = place()
    for o in range(2):
        for part in range(3):
            wide[o * SENT : (o + 1) * SENT, 4 * part : 4 * part + 4, :] = both_ref[o * SENT : (o + 1) * SENT, part].astype(F32)
    flat = wide.reshape(2 * SENT * ROWS, 128)
    lane = iota((CHIPS, 128), 1)

    def row_of(core, source, row):
        return flat[pl.ds((core * SENT + source * CHIPS) * ROWS + row, CHIPS, stride=ROWS), :]

    for t in range(GROUPS):
        for half in range(2):
            align[pl.ds(half * 128 + t, CHIPS, stride=4), :] = row_of(c, t, 10 + half)
    for s in range(CHIPS):
        for half in range(2):
            rows = align[half * 128 + 4 * s : half * 128 + 4 * s + 4, :]
            align_ref[s, :, half * 128 : (half + 1) * 128] = rows.astype(BF16)

    rights, right_masks, lefts = [], [], [jnp.zeros((CHIPS, 128), F32)] * 2
    for t in range(GROUPS):
        rights.append(row_of(c, t, 8))
        mask_row = row_of(c, t, 9)
        right_masks.append(pltpu.roll(mask_row, (128 - 8 * ((t + 1) % 4)) % 128, 1))
        for o in range(2):
            lefts[o] = jnp.where((lane // 8) % 4 == t, row_of(o, t, 9), lefts[o])
    right, right_mask, left_mask = [], [], []
    for s in range(GROUPS):
        of_right, of_mask = jnp.zeros((CHIPS, 128), F32), jnp.zeros((CHIPS, 128), F32)
        for t in range(GROUPS):
            shift = (32 * (t - s)) % 128
            of_right = jnp.where(lane // 32 == t, pltpu.roll(rights[t], shift, 1), of_right)
            of_mask = jnp.where(lane // 32 == t, pltpu.roll(right_masks[t], shift, 1), of_mask)
        right.append(of_right)
        right_mask.append(of_mask)
        left_mask.append(
            jnp.where(
                lane < 32,
                pltpu.roll(lefts[0], (-32 * s) % 128, 1),
                jnp.where(lane < 64, pltpu.roll(lefts[1], (32 - 32 * s) % 128, 1), 0.0),
            )
        )
    right, right_mask, left_mask = (
        jnp.concatenate(rows, axis=0) for rows in (right, right_mask, left_mask)
    )
    counts = dot_tn(left_mask.astype(BF16), right_mask.astype(BF16))

    right = right.astype(BF16)
    for o in range(2):
        for t in range(GROUPS):
            for half in range(2):
                slab = (o * GROUPS + t) * 2 + half
                left = jnp.concatenate([row_of(o, t, 2 * s + half) for s in range(GROUPS)], axis=0).astype(BF16)
                product[slab * 128 : (slab + 1) * 128, :] = dot_tn(left, right)

    block = iota((64, 128), 1) // 32
    total = jnp.zeros((256, 128), F32)
    for n in range(8):
        given = [product[pl.ds(4 * n + m, 64, stride=32), :] for m in range(4)]
        turned = []
        for j in range(4):
            tile = given[j]
            for m in range(4):
                if m != j:
                    tile = jnp.where(block == m, pltpu.roll(given[m], (32 * (m - j)) % 128, 1), tile)
            turned.append(tile.astype(BF16))
        total = total + dot(jnp.concatenate(turned, axis=0), weight_ref[n * 128 : (n + 1) * 128, :])

    for o in range(2):
        for t in range(GROUPS):
            first = (o * GROUPS + t) * 8
            for j in range(4):
                value = total[j * 64 + first : j * 64 + first + 8] / counts[first : first + 8, 32 * j : 32 * j + 1]
                update[pl.ds((4 * o + t) * 4 + j, 8, stride=32), :] = value

    row, column = iota((256, 256), 0), iota((256, 256), 1)
    resolved = jnp.broadcast_to(resolved_ref[...].astype(F32), (128, 256)).astype(BF16)
    row_mask = dot_nt(one_hot(column == 64 * g + row // 4), resolved)
    column_mask = dot_nt(one_hot(column == 8 * k + 4 * c + row % 4), resolved)
    update[...] = row_mask * column_mask * update[...]
    for i in range(64):
        out_ref[i] = (pair_ref[i].astype(F32) + update[4 * i : 4 * i + 4, :]).astype(BF16)


def call(kernel, shapes, scratch, flops, size, interpret, **more):
    return pl.pallas_call(
        kernel,
        out_shape=shapes,
        scratch_shapes=scratch,
        compiler_params=pltpu.CompilerParams(vmem_limit_bytes=VMEM_LIMIT),
        cost_estimate=pl.CostEstimate(flops=flops, bytes_accessed=size, transcendentals=0),
        interpret=interpret,
        **more,
    )


def pack(x, mask, pair, weight, interpret=False):
    arrays = (x, mask.T, pair, weight.T)
    scratch = [pltpu.VMEM(a.shape, a.dtype) for a in arrays]
    scratch += [
        pltpu.VMEM((CHIPS, ROWS, 128), F32),
        pltpu.VMEM((256, 128), F32),
        pltpu.SemaphoreType.DMA((4,)),
    ]
    specs = [pl.BlockSpec(memory_space=pltpu.HBM)] * 4
    if not interpret:
        arrays = [pltpu.with_memory_space_constraint(a, pltpu.HBM) for a in arrays]
    shape = jax.ShapeDtypeStruct((SENT, 13, 128), BF16)
    return call(pack_kernel, shape, scratch, 10**7, 10**6, interpret, in_specs=specs)(*arrays)


def attend(place, own, other, weight, final, sides, interpret=False):
    scratch = [pltpu.VMEM((2 * SENT, ROWS, 128), F32), pltpu.VMEM((CHIPS, ROWS, 128), F32)]
    shape = jax.ShapeDtypeStruct((SENT, 3, 4, 128), BF16)
    kernel = functools.partial(attend_kernel, place)
    return call(kernel, shape, scratch, 10**9, 2 * 10**6, interpret)(own, other, weight, final, sides.T)


def outer(place, both, pair, resolved, weight, interpret=False):
    scratch = [
        pltpu.VMEM((2 * SENT, ROWS, 128), F32),
        pltpu.VMEM((256, 128), F32),
        pltpu.VMEM((2048, 128), F32),
        pltpu.VMEM((256, 128), F32),
    ]
    shapes = (jax.ShapeDtypeStruct((CHIPS, 4, 256), BF16), jax.ShapeDtypeStruct((64, 4, 128), BF16))
    kernel = functools.partial(outer_kernel, place)
    return call(kernel, shapes, scratch, 10**9, 2 * 10**6, interpret)(both, pair, resolved.reshape(1, 256), weight)


def my_place():
    return lax.axis_index("seq"), lax.axis_index("chip"), lax.axis_index("core")


def exchange(messages):
    return lax.all_to_all(messages, ("seq", "chip"), 0, 0, tiled=True)


def per_device(x, mask, resolved, pair, combined, bias_weight, final, sides, outer_weight):
    own = exchange(pack(x, mask, pair, bias_weight))
    other = lax.ppermute(own, "core", [(0, 1), (1, 0)])
    second = exchange(attend(my_place, own, other, combined, final, sides))
    both = lax.all_gather(second, "core", axis=0, tiled=True)
    return outer(my_place, both, pair, resolved, outer_weight)


def solution(mesh):
    crop, seq, res = (mesh.shape[a] for a in ("crop", "seq", "res"))
    fine = Mesh(mesh.devices.reshape(crop, seq, res // 2, 2), ("crop", "seq", "chip", "core"))
    rows, columns = ("crop", "seq"), ("chip", "core")
    placed = (P(rows, columns, None), P(rows, columns), P("crop"), P(rows, columns, None)) + (P(),) * 5
    return jax.shard_map(
        per_device,
        mesh=fine,
        in_specs=placed,
        out_specs=(P(rows, columns, None), P(rows, columns, None)),
        check_vma=False,
    )
```

```python
import functools

import jax
import jax.numpy as jnp
from jax import lax
from jax.experimental import pallas as pl
from jax.experimental.pallas import tpu as pltpu
from jax.sharding import Mesh
from jax.sharding import PartitionSpec as P


F32 = jnp.float32
BF16 = jnp.bfloat16
HEADS, DIM = 8, 32
GROUPS, CHIPS, ROWS = 4, 32, 16
SENT = GROUPS * CHIPS
EPSILON = 1e-5
VMEM_LIMIT = 40 * 2**20


def iota(shape, dim):
    return lax.broadcasted_iota(jnp.int32, shape, dim)


def one_hot(condition):
    return jnp.where(condition, 1.0, 0.0).astype(BF16)


def dot(a, b):
    return jnp.dot(a, b, preferred_element_type=F32)


def dot_nt(a, b):
    return lax.dot_general(a, b, (((1,), (1,)), ((), ())), preferred_element_type=F32)


def dot_tn(a, b):
    return lax.dot_general(a, b, (((0,), (0,)), ((), ())), preferred_element_type=F32)


def standardized(*parts):
    count = sum(p.shape[-1] for p in parts)
    average = jnp.sum(sum(parts[1:], parts[0]), axis=-1, keepdims=True) * (1.0 / count)
    centered = [p - average for p in parts]
    squares = [d * d for d in centered]
    variance = jnp.sum(sum(squares[1:], squares[0]), axis=-1, keepdims=True) * (1.0 / count)
    scale = lax.rsqrt(variance + EPSILON)
    return [d * scale for d in centered]


def pack_kernel(x_hbm, mask_hbm, pair_hbm, weight_hbm, out_ref, x_ref, mask_ref, pair_ref, weight_ref, message, pair_rows, arrived):
    copies = [
        pltpu.make_async_copy(source, to, arrived.at[n])
        for n, (source, to) in enumerate(
            [(pair_hbm, pair_ref), (x_hbm, x_ref), (weight_hbm, weight_ref), (mask_hbm, mask_ref)]
        )
    ]
    for copy in copies:
        copy.start()
    for copy in copies:
        copy.wait()
    (normed,) = standardized(pair_ref[...].astype(F32))
    for i in range(pair_ref.shape[0]):
        pair_rows[4 * i : 4 * i + 4, :] = normed[i]
    spread = one_hot(iota((HEADS, 128), 0) == (iota((HEADS, 128), 1) // 8) % 8)
    weight = dot_tn(weight_ref[...], spread).astype(BF16)
    bias = dot(pair_rows[...].astype(BF16), weight)
    row, lane = iota((256, 128), 0), iota((256, 128), 1)
    own = (row // 32 == lane % 8) & ((row // 16) % 2 == lane // 64)
    bias = jnp.sum(jnp.where(own, bias, 0.0).reshape(16, 16, 128), axis=0)

    x = x_ref[...].astype(F32)
    message[:, 0:4, :] = x[:, :, :128]
    message[:, 8:12, :] = x[:, :, 128:]
    mask = mask_ref[...].astype(F32).astype(BF16)
    flat = message.reshape(CHIPS * ROWS, 128)
    flat[pl.ds(12, CHIPS, stride=ROWS), :] = dot_tn(mask, one_hot(iota((4, 128), 0) == iota((4, 128), 1) // 32))
    for g in range(GROUPS):
        message[:, 4:8, :] = jnp.broadcast_to(bias[4 * g : 4 * g + 4][None], (CHIPS, 4, 128))
        out_ref[g * CHIPS : (g + 1) * CHIPS] = message[:, 0:13, :].astype(BF16)


def keys_of(ref, wide, weight_ref, c):
    low = iota((16, 8, 128), 1) < 4
    lane = iota((128, 128), 1)

    def first_halves(tiles):
        return jnp.where(low, tiles[:16], pltpu.roll(tiles[16:], 4, 1)).reshape(128, 128)

    def second_halves(tiles):
        return jnp.where(low, pltpu.roll(tiles[:16], 4, 1), tiles[16:]).reshape(128, 128)

    flat = wide.reshape(SENT * ROWS, 128)
    normed, masks, biases = [], [], []
    for s in range(GROUPS):
        mine = slice(s * CHIPS, (s + 1) * CHIPS)
        wide[mine, 0:13, :] = ref[mine].astype(F32)
        tiles = wide[mine, 0:8, :]
        x0, x1 = first_halves(tiles), first_halves(wide[mine, 8:16, :])
        normed.append(jnp.concatenate(standardized(x0, x1), axis=1).astype(BF16))
        masks.append(flat[pl.ds(s * CHIPS * ROWS + 12, CHIPS, stride=ROWS), :])
        bias = second_halves(tiles)
        biases.append(jnp.where(c == 0, bias, pltpu.roll(bias, 64, 1)))
    key_value = dot(jnp.concatenate(normed, axis=0), weight_ref[:, 256:768]).astype(BF16)
    bias = jnp.concatenate(
        [
            jnp.where(lane < 64, biases[2 * n], pltpu.roll(biases[2 * n + 1], 64, 1)).T
            for n in range(2)
        ],
        axis=0,
    )
    masks = jnp.concatenate(masks, axis=0).astype(BF16)
    spread = dot(masks, one_hot(iota((128, 128), 0) == 32 * (lane % 4))).reshape(GROUPS, CHIPS, 128)
    chip, key = iota((GROUPS, CHIPS, 128), 1), iota((GROUPS, CHIPS, 128), 2)
    rows = jnp.sum(jnp.where(chip == key // 8 + 16 * ((key // 4) % 2), spread, 0.0), axis=1)
    return key_value, bias, rows, masks


def first_kernel(
    place, own_ref, weight_ref, key_value_ref, query_ref, gate_ref, residual_ref, present_ref, bias_ref, mask_ref, wide
):
    g, _, c = place()
    key_value_ref[...], bias_ref[...], mask_ref[...], masks = keys_of(own_ref, wide, weight_ref, c)
    flat = wide.reshape(SENT * ROWS, 128)
    x0, x1 = (
        jnp.concatenate(
            [flat[pl.ds(s * CHIPS * ROWS + row + g, CHIPS, stride=ROWS), :] for s in range(GROUPS)], axis=0
        )
        for row in (0, 8)
    )
    residual_ref[...] = jnp.concatenate([x0, x1], axis=1)
    normed = jnp.concatenate(standardized(x0, x1), axis=1).astype(BF16)
    query_ref[...] = (dot(normed, weight_ref[:, :256]) * DIM**-0.5).astype(BF16)
    gate_ref[...] = jax.nn.sigmoid(dot(normed, weight_ref[:, 768:]))
    present_ref[...] = dot(masks, one_hot(iota((128, 128), 0) == 32 * g))


def attend_kernel(
    place,
    other_ref,
    key_value_ref,
    query_ref,
    gate_ref,
    residual_ref,
    present_ref,
    bias_ref,
    mask_ref,
    weight_ref,
    final_ref,
    sides_ref,
    out_ref,
    wide,
    message,
):
    g, _, c = place()
    lane = iota((128, 128), 1)
    key_value, bias, masks, _ = keys_of(other_ref, wide, weight_ref, c)
    pair_bias = jnp.concatenate([bias_ref[...], bias], axis=1)
    masks = (jnp.concatenate([mask_ref[...], masks], axis=1) - 1.0) * 1e9
    of_head = jnp.where(
        iota((HEADS, 8, 256), 2) // DIM == iota((HEADS, 8, 256), 0), 1.0, 0.0
    )
    gated = []
    for s in range(GROUPS):
        mine, half = slice(s * CHIPS, (s + 1) * CHIPS), slice(s * 128, (s + 1) * 128)
        keys = jnp.concatenate([key_value_ref[half, :256], key_value[half, :256]], axis=0)
        values = jnp.concatenate([key_value_ref[half, 256:], key_value[half, 256:]], axis=0)
        spread = query_ref[mine, :].astype(F32).reshape(GROUPS, 1, 8, 256) * of_head[None]
        scores = dot_nt(spread.reshape(256, 256).astype(BF16), keys) + pair_bias + masks[s : s + 1]
        exponent = jnp.exp(scores - jnp.max(scores, axis=-1, keepdims=True))
        weights = (exponent * (1.0 / jnp.sum(exponent, axis=-1, keepdims=True))).astype(BF16)
        mixed = dot(weights, values).reshape(GROUPS, HEADS, 8, 256) * of_head[None]
        attended = jnp.sum(mixed, axis=1).reshape(CHIPS, 256).astype(BF16)
        gated.append((gate_ref[mine, :] * attended.astype(F32)).astype(BF16))
    present = present_ref[...]

    result = residual_ref[...] + dot(jnp.concatenate(gated, axis=0), final_ref[...])
    result = result.astype(BF16).astype(F32)
    (normed_out,) = standardized(result)
    entry, place_of = iota((64, 256), 0), iota((64, 256), 1)
    four_times = one_hot(entry == (place_of // 128) * 32 + place_of % 32)
    sides = dot(normed_out.astype(BF16), dot_tn(sides_ref[...], four_times).astype(BF16))
    left = (sides[:, :128] * present).astype(BF16)
    right = (sides[:, 128:] * present).astype(BF16).astype(F32)

    new, old = iota((128, 128), 0), iota((128, 128), 1)
    moved = one_hot(
        old == ((new // 2) % 4) * 32 + ((new // 8) % 4) * 8 + (new % 2) * 4 + new // 32
    )
    left = jnp.where(lane // 32 == new // 32, dot(moved, left), 0.0)
    left = jnp.sum(left.reshape(4, 32, 128), axis=0)
    row = new
    left_mask = jnp.where(lane == 32 * (row // 32) + 8 * g + row % 8, present, 0.0).astype(BF16)
    left_mask = dot(one_hot((iota((8, 128), 1) // 8) % 4 == iota((8, 128), 0)), left_mask)
    sequence = iota((CHIPS, 128), 1) // 32
    right_at = (iota((CHIPS, 128), 1) // 8) % 4 == (g + 1) % 4
    right_row, mask_row = jnp.zeros((CHIPS, 128), F32), jnp.zeros((CHIPS, 128), F32)
    for s in range(GROUPS):
        mine = slice(s * CHIPS, (s + 1) * CHIPS)
        right_row = jnp.where(sequence == s, right[mine], right_row)
        mask_row = jnp.where((sequence == s) & right_at, present[mine], mask_row)

    flat = message.reshape(CHIPS * 8, 128)
    flat[pl.ds(0, CHIPS, stride=8), :] = right_row
    for n in range(GROUPS):
        to = slice(n * CHIPS, (n + 1) * CHIPS)
        for part in range(2):
            rows = left[8 * n + 4 * part : 8 * n + 4 * part + 4].astype(BF16)
            out_ref[to, part] = jnp.broadcast_to(rows[None], (CHIPS, 4, 128))
        flat[pl.ds(1, CHIPS, stride=8), :] = mask_row + left_mask[n : n + 1]
        for half in range(2):
            flat[pl.ds(2 + half, CHIPS, stride=8), :] = result[to, half * 128 : (half + 1) * 128]
        out_ref[to, 2] = message[:, 0:4, :].astype(BF16)


def outer_kernel(
    place, both_ref, pair_ref, resolved_hbm, weight_ref, align_ref, out_ref, wide, align, product, update, resolved_ref, arrived
):
    g, k, c = place()
    copy = pltpu.make_async_copy(resolved_hbm, resolved_ref, arrived)
    copy.start()
    for o in range(2):
        for part in range(3):
            wide[o * SENT : (o + 1) * SENT, 4 * part : 4 * part + 4, :] = both_ref[o * SENT : (o + 1) * SENT, part].astype(F32)
    flat = wide.reshape(2 * SENT * ROWS, 128)
    lane = iota((CHIPS, 128), 1)

    def row_of(core, source, row):
        return flat[pl.ds((core * SENT + source * CHIPS) * ROWS + row, CHIPS, stride=ROWS), :]

    for t in range(GROUPS):
        for half in range(2):
            align[pl.ds(half * 128 + t, CHIPS, stride=4), :] = row_of(c, t, 10 + half)
    for s in range(CHIPS):
        for half in range(2):
            rows = align[half * 128 + 4 * s : half * 128 + 4 * s + 4, :]
            align_ref[s, :, half * 128 : (half + 1) * 128] = rows.astype(BF16)

    rights, right_masks, lefts = [], [], [jnp.zeros((CHIPS, 128), F32)] * 2
    for t in range(GROUPS):
        rights.append(row_of(c, t, 8))
        mask_row = row_of(c, t, 9)
        right_masks.append(pltpu.roll(mask_row, (128 - 8 * ((t + 1) % 4)) % 128, 1))
        for o in range(2):
            lefts[o] = jnp.where((lane // 8) % 4 == t, row_of(o, t, 9), lefts[o])
    right, right_mask, left_mask = [], [], []
    for s in range(GROUPS):
        of_right, of_mask = jnp.zeros((CHIPS, 128), F32), jnp.zeros((CHIPS, 128), F32)
        for t in range(GROUPS):
            shift = (32 * (t - s)) % 128
            of_right = jnp.where(lane // 32 == t, pltpu.roll(rights[t], shift, 1), of_right)
            of_mask = jnp.where(lane // 32 == t, pltpu.roll(right_masks[t], shift, 1), of_mask)
        right.append(of_right)
        right_mask.append(of_mask)
        left_mask.append(
            jnp.where(
                lane < 32,
                pltpu.roll(lefts[0], (-32 * s) % 128, 1),
                jnp.where(lane < 64, pltpu.roll(lefts[1], (32 - 32 * s) % 128, 1), 0.0),
            )
        )
    right, right_mask, left_mask = (
        jnp.concatenate(rows, axis=0) for rows in (right, right_mask, left_mask)
    )
    counts = dot_tn(left_mask.astype(BF16), right_mask.astype(BF16))

    right = right.astype(BF16)
    for o in range(2):
        for t in range(GROUPS):
            for half in range(2):
                slab = (o * GROUPS + t) * 2 + half
                left = jnp.concatenate([row_of(o, t, 2 * s + half) for s in range(GROUPS)], axis=0).astype(BF16)
                product[slab * 128 : (slab + 1) * 128, :] = dot_tn(left, right)

    block = iota((64, 128), 1) // 32
    total = jnp.zeros((256, 128), F32)
    for n in range(8):
        given = [product[pl.ds(4 * n + m, 64, stride=32), :] for m in range(4)]
        turned = []
        for j in range(4):
            tile = given[j]
            for m in range(4):
                if m != j:
                    tile = jnp.where(block == m, pltpu.roll(given[m], (32 * (m - j)) % 128, 1), tile)
            turned.append(tile.astype(BF16))
        total = total + dot(jnp.concatenate(turned, axis=0), weight_ref[n * 128 : (n + 1) * 128, :])

    for o in range(2):
        for t in range(GROUPS):
            first = (o * GROUPS + t) * 8
            for j in range(4):
                value = total[j * 64 + first : j * 64 + first + 8] / counts[first : first + 8, 32 * j : 32 * j + 1]
                update[pl.ds((4 * o + t) * 4 + j, 8, stride=32), :] = value

    copy.wait()
    row, column = iota((256, 256), 0), iota((256, 256), 1)
    resolved = jnp.broadcast_to(resolved_ref[...].astype(F32), (128, 256)).astype(BF16)
    row_mask = dot_nt(one_hot(column == 64 * g + row // 4), resolved)
    column_mask = dot_nt(one_hot(column == 8 * k + 4 * c + row % 4), resolved)
    update[...] = row_mask * column_mask * update[...]
    for i in range(64):
        out_ref[i] = (pair_ref[i].astype(F32) + update[4 * i : 4 * i + 4, :]).astype(BF16)


def call(kernel, shapes, scratch, flops, size, interpret, **more):
    return pl.pallas_call(
        kernel,
        out_shape=shapes,
        scratch_shapes=scratch,
        compiler_params=pltpu.CompilerParams(vmem_limit_bytes=VMEM_LIMIT),
        cost_estimate=pl.CostEstimate(flops=flops, bytes_accessed=size, transcendentals=0),
        interpret=interpret,
        **more,
    )


def pack(x, mask, pair, weight, interpret=False):
    arrays = (x, mask.T, pair, weight.T)
    scratch = [pltpu.VMEM(a.shape, a.dtype) for a in arrays]
    scratch += [
        pltpu.VMEM((CHIPS, ROWS, 128), F32),
        pltpu.VMEM((256, 128), F32),
        pltpu.SemaphoreType.DMA((4,)),
    ]
    specs = [pl.BlockSpec(memory_space=pltpu.HBM)] * 4
    if not interpret:
        arrays = [pltpu.with_memory_space_constraint(a, pltpu.HBM) for a in arrays]
    shape = jax.ShapeDtypeStruct((SENT, 13, 128), BF16)
    return call(pack_kernel, shape, scratch, 10**7, 10**6, interpret, in_specs=specs)(*arrays)


def first(place, own, weight, interpret=False):
    kernel = functools.partial(first_kernel, place)
    shapes = [
        jax.ShapeDtypeStruct(shape, dtype)
        for shape, dtype in [
            ((512, 512), BF16),
            ((128, 256), BF16),
            ((128, 256), F32),
            ((128, 256), F32),
            ((128, 128), F32),
            ((256, 128), F32),
            ((GROUPS, 128), F32),
        ]
    ]
    scratch = [pltpu.VMEM((SENT, ROWS, 128), F32)]
    return call(kernel, shapes, scratch, 10**9, 2 * 10**6, interpret)(own, weight)


def attend(place, other, mine, weight, final, sides, interpret=False):
    scratch = [pltpu.VMEM((SENT, ROWS, 128), F32), pltpu.VMEM((CHIPS, 8, 128), F32)]
    shape = jax.ShapeDtypeStruct((SENT, 3, 4, 128), BF16)
    kernel = functools.partial(attend_kernel, place)
    return call(kernel, shape, scratch, 10**9, 2 * 10**6, interpret)(other, *mine, weight, final, sides.T)


def outer(place, both, pair, resolved, weight, interpret=False):
    scratch = [
        pltpu.VMEM((2 * SENT, ROWS, 128), F32),
        pltpu.VMEM((256, 128), F32),
        pltpu.VMEM((2048, 128), F32),
        pltpu.VMEM((256, 128), F32),
        pltpu.VMEM((1, 256), jnp.int32),
        pltpu.SemaphoreType.DMA,
    ]
    shapes = (jax.ShapeDtypeStruct((CHIPS, 4, 256), BF16), jax.ShapeDtypeStruct((64, 4, 128), BF16))
    kernel = functools.partial(outer_kernel, place)
    resolved = resolved.reshape(1, 256)
    vmem, hbm = pl.BlockSpec(memory_space=pltpu.VMEM), pl.BlockSpec(memory_space=pltpu.HBM)
    if not interpret:
        resolved = pltpu.with_memory_space_constraint(resolved, pltpu.HBM)
    return call(kernel, shapes, scratch, 10**9, 2 * 10**6, interpret, in_specs=[vmem, vmem, hbm, vmem])(
        both, pair, resolved, weight
    )


def my_place():
    return lax.axis_index("seq"), lax.axis_index("chip"), lax.axis_index("core")


def exchange(messages):
    return lax.all_to_all(messages, ("seq", "chip"), 0, 0, tiled=True)


def per_device(x, mask, resolved, pair, combined, bias_weight, final, sides, outer_weight):
    own = exchange(pack(x, mask, pair, bias_weight))
    other = lax.ppermute(own, "core", [(0, 1), (1, 0)])
    mine = first(my_place, own, combined)
    second = exchange(attend(my_place, other, mine, combined, final, sides))
    both = lax.all_gather(second, "core", axis=0, tiled=True)
    return outer(my_place, both, pair, resolved, outer_weight)


def solution(mesh):
    crop, seq, res = (mesh.shape[a] for a in ("crop", "seq", "res"))
    fine = Mesh(mesh.devices.reshape(crop, seq, res // 2, 2), ("crop", "seq", "chip", "core"))
    rows, columns = ("crop", "seq"), ("chip", "core")
    placed = (P(rows, columns, None), P(rows, columns), P("crop"), P(rows, columns, None)) + (P(),) * 5
    return jax.shard_map(
        per_device,
        mesh=fine,
        in_specs=placed,
        out_specs=(P(rows, columns, None), P(rows, columns, None)),
        check_vma=False,
    )
```

```python
import functools

import jax
import jax.numpy as jnp
from jax import lax
from jax.experimental import pallas as pl
from jax.experimental.pallas import tpu as pltpu
from jax.sharding import Mesh
from jax.sharding import PartitionSpec as P


F32 = jnp.float32
BF16 = jnp.bfloat16
HEADS, DIM = 8, 32
GROUPS, CHIPS, ROWS = 4, 32, 16
SENT = GROUPS * CHIPS
EPSILON = 1e-5
VMEM_LIMIT = 40 * 2**20


def iota(shape, dim):
    return lax.broadcasted_iota(jnp.int32, shape, dim)


def one_hot(condition):
    return jnp.where(condition, 1.0, 0.0).astype(BF16)


def dot(a, b):
    return jnp.dot(a, b, preferred_element_type=F32)


def dot_nt(a, b):
    return lax.dot_general(a, b, (((1,), (1,)), ((), ())), preferred_element_type=F32)


def dot_tn(a, b):
    return lax.dot_general(a, b, (((0,), (0,)), ((), ())), preferred_element_type=F32)


def standardized(*parts):
    count = sum(p.shape[-1] for p in parts)
    average = jnp.sum(sum(parts[1:], parts[0]), axis=-1, keepdims=True) * (1.0 / count)
    centered = [p - average for p in parts]
    squares = [d * d for d in centered]
    variance = jnp.sum(sum(squares[1:], squares[0]), axis=-1, keepdims=True) * (1.0 / count)
    scale = lax.rsqrt(variance + EPSILON)
    return [d * scale for d in centered]


def pack_kernel(x_hbm, mask_hbm, pair_hbm, weight_hbm, out_ref, x_ref, mask_ref, pair_ref, weight_ref, message, pair_rows, arrived):
    copies = [
        pltpu.make_async_copy(source, to, arrived.at[n])
        for n, (source, to) in enumerate(
            [(pair_hbm, pair_ref), (x_hbm, x_ref), (weight_hbm, weight_ref), (mask_hbm, mask_ref)]
        )
    ]
    for copy in copies:
        copy.start()
    for copy in copies:
        copy.wait()
    (normed,) = standardized(pair_ref[...].astype(F32))
    for i in range(pair_ref.shape[0]):
        pair_rows[4 * i : 4 * i + 4, :] = normed[i]
    spread = one_hot(iota((HEADS, 128), 0) == (iota((HEADS, 128), 1) // 8) % 8)
    weight = dot_tn(weight_ref[...], spread).astype(BF16)
    bias = dot(pair_rows[...].astype(BF16), weight)
    row, lane = iota((256, 128), 0), iota((256, 128), 1)
    own = (row // 32 == lane % 8) & ((row // 16) % 2 == lane // 64)
    bias = jnp.sum(jnp.where(own, bias, 0.0).reshape(16, 16, 128), axis=0)

    x = x_ref[...].astype(F32)
    message[:, 0:4, :] = x[:, :, :128]
    message[:, 8:12, :] = x[:, :, 128:]
    mask = mask_ref[...].astype(F32).astype(BF16)
    flat = message.reshape(CHIPS * ROWS, 128)
    flat[pl.ds(12, CHIPS, stride=ROWS), :] = dot_tn(mask, one_hot(iota((4, 128), 0) == iota((4, 128), 1) // 32))
    for g in range(GROUPS):
        message[:, 4:8, :] = jnp.broadcast_to(bias[4 * g : 4 * g + 4][None], (CHIPS, 4, 128))
        out_ref[g * CHIPS : (g + 1) * CHIPS] = message[:, 0:13, :].astype(BF16)


def keys_of(ref, wide, weight_ref, c):
    low = iota((16, 8, 128), 1) < 4
    lane = iota((128, 128), 1)

    def first_halves(tiles):
        return jnp.where(low, tiles[:16], pltpu.roll(tiles[16:], 4, 1)).reshape(128, 128)

    def second_halves(tiles):
        return jnp.where(low, pltpu.roll(tiles[:16], 4, 1), tiles[16:]).reshape(128, 128)

    flat = wide.reshape(SENT * ROWS, 128)
    normed, masks, biases = [], [], []
    for s in range(GROUPS):
        mine = slice(s * CHIPS, (s + 1) * CHIPS)
        wide[mine, 0:13, :] = ref[mine].astype(F32)
        tiles = wide[mine, 0:8, :]
        x0, x1 = first_halves(tiles), first_halves(wide[mine, 8:16, :])
        normed.append(jnp.concatenate(standardized(x0, x1), axis=1).astype(BF16))
        masks.append(flat[pl.ds(s * CHIPS * ROWS + 12, CHIPS, stride=ROWS), :])
        bias = second_halves(tiles)
        biases.append(jnp.where(c == 0, bias, pltpu.roll(bias, 64, 1)))
    key_value = dot(jnp.concatenate(normed, axis=0), weight_ref[:, 256:768]).astype(BF16)
    bias = jnp.concatenate(
        [
            jnp.where(lane < 64, biases[2 * n], pltpu.roll(biases[2 * n + 1], 64, 1)).T
            for n in range(2)
        ],
        axis=0,
    )
    masks = jnp.concatenate(masks, axis=0).astype(BF16)
    spread = dot(masks, one_hot(iota((128, 128), 0) == 32 * (lane % 4))).reshape(GROUPS, CHIPS, 128)
    chip, key = iota((GROUPS, CHIPS, 128), 1), iota((GROUPS, CHIPS, 128), 2)
    rows = jnp.sum(jnp.where(chip == key // 8 + 16 * ((key // 4) % 2), spread, 0.0), axis=1)
    return key_value, bias, rows, masks


def heads():
    return jnp.where(iota((HEADS, 8, 256), 2) // DIM == iota((HEADS, 8, 256), 0), 1.0, 0.0)


def first_kernel(
    place,
    own_ref,
    weight_ref,
    sides_ref,
    resolved_ref,
    value_ref,
    query_ref,
    score_ref,
    gate_ref,
    residual_ref,
    present_ref,
    wide_sides_ref,
    pair_mask_ref,
    wide,
):
    g, k, c = place()
    key_value, bias, key_masks, masks = keys_of(own_ref, wide, weight_ref, c)
    value_ref[...] = key_value[:, 256:]
    flat = wide.reshape(SENT * ROWS, 128)
    x0, x1 = (
        jnp.concatenate(
            [flat[pl.ds(s * CHIPS * ROWS + row + g, CHIPS, stride=ROWS), :] for s in range(GROUPS)], axis=0
        )
        for row in (0, 8)
    )
    residual_ref[...] = jnp.concatenate([x0, x1], axis=1)
    normed = jnp.concatenate(standardized(x0, x1), axis=1).astype(BF16)
    queries = (dot(normed, weight_ref[:, :256]) * DIM**-0.5).astype(BF16).astype(F32)
    of_head = heads()
    for s in range(GROUPS):
        spread = queries[s * CHIPS : (s + 1) * CHIPS].reshape(GROUPS, 1, 8, 256) * of_head[None]
        spread = spread.reshape(256, 256).astype(BF16)
        query_ref[s] = spread
        score_ref[s] = dot_nt(spread, key_value[s * 128 : (s + 1) * 128, :256]) + bias + (key_masks[s : s + 1] - 1.0) * 1e9
    gate_ref[...] = jax.nn.sigmoid(dot(normed, weight_ref[:, 768:]))
    present_ref[...] = dot(masks, one_hot(iota((128, 128), 0) == 32 * g))

    entry, place_of = iota((64, 256), 0), iota((64, 256), 1)
    four_times = one_hot(entry == (place_of // 128) * 32 + place_of % 32)
    wide_sides_ref[...] = dot_tn(sides_ref[...], four_times).astype(BF16)
    row, column = iota((256, 256), 0), iota((256, 256), 1)
    resolved = jnp.broadcast_to(resolved_ref[...].astype(F32), (128, 256)).astype(BF16)
    row_mask = dot_nt(one_hot(column == 64 * g + row // 4), resolved)
    pair_mask_ref[...] = row_mask * dot_nt(one_hot(column == 8 * k + 4 * c + row % 4), resolved)


def attend_kernel(
    place,
    other_ref,
    value_ref,
    query_ref,
    score_ref,
    gate_ref,
    residual_ref,
    present_ref,
    wide_sides_ref,
    weight_ref,
    final_ref,
    out_ref,
    wide,
    message,
):
    g, _, c = place()
    lane = iota((128, 128), 1)
    key_value, bias, masks, _ = keys_of(other_ref, wide, weight_ref, c)
    of_head = heads()
    gated = []
    for s in range(GROUPS):
        mine, half = slice(s * CHIPS, (s + 1) * CHIPS), slice(s * 128, (s + 1) * 128)
        values = jnp.concatenate([value_ref[half, :], key_value[half, 256:]], axis=0)
        scores = dot_nt(query_ref[s], key_value[half, :256]) + bias + (masks[s : s + 1] - 1.0) * 1e9
        scores = jnp.concatenate([score_ref[s], scores], axis=1)
        exponent = jnp.exp(scores - jnp.max(scores, axis=-1, keepdims=True))
        weights = (exponent * (1.0 / jnp.sum(exponent, axis=-1, keepdims=True))).astype(BF16)
        mixed = dot(weights, values).reshape(GROUPS, HEADS, 8, 256) * of_head[None]
        attended = jnp.sum(mixed, axis=1).reshape(CHIPS, 256).astype(BF16)
        gated.append((gate_ref[mine, :] * attended.astype(F32)).astype(BF16))
    present = present_ref[...]

    result = residual_ref[...] + dot(jnp.concatenate(gated, axis=0), final_ref[...])
    result = result.astype(BF16).astype(F32)
    (normed_out,) = standardized(result)
    sides = dot(normed_out.astype(BF16), wide_sides_ref[...])
    left = (sides[:, :128] * present).astype(BF16)
    right = (sides[:, 128:] * present).astype(BF16).astype(F32)

    new, old = iota((128, 128), 0), iota((128, 128), 1)
    moved = one_hot(
        old == ((new // 2) % 4) * 32 + ((new // 8) % 4) * 8 + (new % 2) * 4 + new // 32
    )
    left = jnp.where(lane // 32 == new // 32, dot(moved, left), 0.0)
    left = jnp.sum(left.reshape(4, 32, 128), axis=0)
    row = new
    left_mask = jnp.where(lane == 32 * (row // 32) + 8 * g + row % 8, present, 0.0).astype(BF16)
    left_mask = dot(one_hot((iota((8, 128), 1) // 8) % 4 == iota((8, 128), 0)), left_mask)
    sequence = iota((CHIPS, 128), 1) // 32
    right_at = (iota((CHIPS, 128), 1) // 8) % 4 == (g + 1) % 4
    right_row, mask_row = jnp.zeros((CHIPS, 128), F32), jnp.zeros((CHIPS, 128), F32)
    for s in range(GROUPS):
        mine = slice(s * CHIPS, (s + 1) * CHIPS)
        right_row = jnp.where(sequence == s, right[mine], right_row)
        mask_row = jnp.where((sequence == s) & right_at, present[mine], mask_row)

    flat = message.reshape(CHIPS * 8, 128)
    flat[pl.ds(0, CHIPS, stride=8), :] = right_row
    for n in range(GROUPS):
        to = slice(n * CHIPS, (n + 1) * CHIPS)
        for part in range(2):
            rows = left[8 * n + 4 * part : 8 * n + 4 * part + 4].astype(BF16)
            out_ref[to, part] = jnp.broadcast_to(rows[None], (CHIPS, 4, 128))
        flat[pl.ds(1, CHIPS, stride=8), :] = mask_row + left_mask[n : n + 1]
        for half in range(2):
            flat[pl.ds(2 + half, CHIPS, stride=8), :] = result[to, half * 128 : (half + 1) * 128]
        out_ref[to, 2] = message[:, 0:4, :].astype(BF16)


def outer_kernel(
    place, both_ref, pair_ref, mask_ref, weight_ref, align_hbm, out_ref, wide, align, product, update, align_ref, left_here
):
    _, _, c = place()
    for o in range(2):
        for part in range(3):
            wide[o * SENT : (o + 1) * SENT, 4 * part : 4 * part + 4, :] = both_ref[o * SENT : (o + 1) * SENT, part].astype(F32)
    flat = wide.reshape(2 * SENT * ROWS, 128)
    lane = iota((CHIPS, 128), 1)

    def row_of(core, source, row):
        return flat[pl.ds((core * SENT + source * CHIPS) * ROWS + row, CHIPS, stride=ROWS), :]

    for t in range(GROUPS):
        for half in range(2):
            align[pl.ds(half * 128 + t, CHIPS, stride=4), :] = row_of(c, t, 10 + half)
    for s in range(CHIPS):
        for half in range(2):
            rows = align[half * 128 + 4 * s : half * 128 + 4 * s + 4, :]
            align_ref[s, :, half * 128 : (half + 1) * 128] = rows.astype(BF16)
    copy = pltpu.make_async_copy(align_ref, align_hbm, left_here)
    copy.start()

    rights, right_masks, lefts = [], [], [jnp.zeros((CHIPS, 128), F32)] * 2
    for t in range(GROUPS):
        rights.append(row_of(c, t, 8))
        mask_row = row_of(c, t, 9)
        right_masks.append(pltpu.roll(mask_row, (128 - 8 * ((t + 1) % 4)) % 128, 1))
        for o in range(2):
            lefts[o] = jnp.where((lane // 8) % 4 == t, row_of(o, t, 9), lefts[o])
    right, right_mask, left_mask = [], [], []
    for s in range(GROUPS):
        of_right, of_mask = jnp.zeros((CHIPS, 128), F32), jnp.zeros((CHIPS, 128), F32)
        for t in range(GROUPS):
            shift = (32 * (t - s)) % 128
            of_right = jnp.where(lane // 32 == t, pltpu.roll(rights[t], shift, 1), of_right)
            of_mask = jnp.where(lane // 32 == t, pltpu.roll(right_masks[t], shift, 1), of_mask)
        right.append(of_right)
        right_mask.append(of_mask)
        left_mask.append(
            jnp.where(
                lane < 32,
                pltpu.roll(lefts[0], (-32 * s) % 128, 1),
                jnp.where(lane < 64, pltpu.roll(lefts[1], (32 - 32 * s) % 128, 1), 0.0),
            )
        )
    right, right_mask, left_mask = (
        jnp.concatenate(rows, axis=0) for rows in (right, right_mask, left_mask)
    )
    counts = dot_tn(left_mask.astype(BF16), right_mask.astype(BF16))

    right = right.astype(BF16)
    for o in range(2):
        for t in range(GROUPS):
            for half in range(2):
                slab = (o * GROUPS + t) * 2 + half
                left = jnp.concatenate([row_of(o, t, 2 * s + half) for s in range(GROUPS)], axis=0).astype(BF16)
                product[slab * 128 : (slab + 1) * 128, :] = dot_tn(left, right)

    block = iota((64, 128), 1) // 32
    total = jnp.zeros((256, 128), F32)
    for n in range(8):
        given = [product[pl.ds(4 * n + m, 64, stride=32), :] for m in range(4)]
        turned = []
        for j in range(4):
            tile = given[j]
            for m in range(4):
                if m != j:
                    tile = jnp.where(block == m, pltpu.roll(given[m], (32 * (m - j)) % 128, 1), tile)
            turned.append(tile.astype(BF16))
        total = total + dot(jnp.concatenate(turned, axis=0), weight_ref[n * 128 : (n + 1) * 128, :])

    for o in range(2):
        for t in range(GROUPS):
            first = (o * GROUPS + t) * 8
            for j in range(4):
                value = total[j * 64 + first : j * 64 + first + 8] / counts[first : first + 8, 32 * j : 32 * j + 1]
                update[pl.ds((4 * o + t) * 4 + j, 8, stride=32), :] = value

    update[...] = mask_ref[...] * update[...]
    for i in range(64):
        out_ref[i] = (pair_ref[i].astype(F32) + update[4 * i : 4 * i + 4, :]).astype(BF16)
    copy.wait()


def call(kernel, shapes, scratch, flops, size, interpret, **more):
    return pl.pallas_call(
        kernel,
        out_shape=shapes,
        scratch_shapes=scratch,
        compiler_params=pltpu.CompilerParams(vmem_limit_bytes=VMEM_LIMIT),
        cost_estimate=pl.CostEstimate(flops=flops, bytes_accessed=size, transcendentals=0),
        interpret=interpret,
        **more,
    )


def pack(x, mask, pair, weight, interpret=False):
    arrays = (x, mask.T, pair, weight.T)
    scratch = [pltpu.VMEM(a.shape, a.dtype) for a in arrays]
    scratch += [
        pltpu.VMEM((CHIPS, ROWS, 128), F32),
        pltpu.VMEM((256, 128), F32),
        pltpu.SemaphoreType.DMA((4,)),
    ]
    specs = [pl.BlockSpec(memory_space=pltpu.HBM)] * 4
    if not interpret:
        arrays = [pltpu.with_memory_space_constraint(a, pltpu.HBM) for a in arrays]
    shape = jax.ShapeDtypeStruct((SENT, 13, 128), BF16)
    return call(pack_kernel, shape, scratch, 10**7, 10**6, interpret, in_specs=specs)(*arrays)


def first(place, own, weight, sides, resolved, interpret=False):
    kernel = functools.partial(first_kernel, place)
    shapes = [
        jax.ShapeDtypeStruct(shape, dtype)
        for shape, dtype in [
            ((512, 256), BF16),
            ((GROUPS, 256, 256), BF16),
            ((GROUPS, 256, 128), F32),
            ((128, 256), F32),
            ((128, 256), F32),
            ((128, 128), F32),
            ((256, 256), BF16),
            ((256, 128), F32),
        ]
    ]
    scratch = [pltpu.VMEM((SENT, ROWS, 128), F32)]
    return call(kernel, shapes, scratch, 10**9, 2 * 10**6, interpret)(
        own, weight, sides.T, resolved.reshape(1, 256)
    )


def attend(place, other, mine, weight, final, interpret=False):
    scratch = [pltpu.VMEM((SENT, ROWS, 128), F32), pltpu.VMEM((CHIPS, 8, 128), F32)]
    shape = jax.ShapeDtypeStruct((SENT, 3, 4, 128), BF16)
    kernel = functools.partial(attend_kernel, place)
    return call(kernel, shape, scratch, 10**9, 2 * 10**6, interpret)(other, *mine, weight, final)


def outer(place, both, pair, pair_mask, weight, interpret=False):
    scratch = [
        pltpu.VMEM((2 * SENT, ROWS, 128), F32),
        pltpu.VMEM((256, 128), F32),
        pltpu.VMEM((2048, 128), F32),
        pltpu.VMEM((256, 128), F32),
        pltpu.VMEM((CHIPS, 4, 256), BF16),
        pltpu.SemaphoreType.DMA,
    ]
    shapes = (jax.ShapeDtypeStruct((CHIPS, 4, 256), BF16), jax.ShapeDtypeStruct((64, 4, 128), BF16))
    kernel = functools.partial(outer_kernel, place)
    specs = (pl.BlockSpec(memory_space=pltpu.HBM), pl.BlockSpec(memory_space=pltpu.VMEM))
    return call(kernel, shapes, scratch, 10**9, 2 * 10**6, interpret, out_specs=specs)(both, pair, pair_mask, weight)


def my_place():
    return lax.axis_index("seq"), lax.axis_index("chip"), lax.axis_index("core")


def exchange(messages):
    return lax.all_to_all(messages, ("seq", "chip"), 0, 0, tiled=True)


def per_device(x, mask, resolved, pair, combined, bias_weight, final, sides, outer_weight):
    own = exchange(pack(x, mask, pair, bias_weight))
    other = lax.ppermute(own, "core", [(0, 1), (1, 0)])
    *mine, pair_mask = first(my_place, own, combined, sides, resolved)
    second = exchange(attend(my_place, other, mine, combined, final))
    both = lax.all_gather(second, "core", axis=0, tiled=True)
    return outer(my_place, both, pair, pair_mask, outer_weight)


def solution(mesh):
    crop, seq, res = (mesh.shape[a] for a in ("crop", "seq", "res"))
    fine = Mesh(mesh.devices.reshape(crop, seq, res // 2, 2), ("crop", "seq", "chip", "core"))
    rows, columns = ("crop", "seq"), ("chip", "core")
    placed = (P(rows, columns, None), P(rows, columns), P("crop"), P(rows, columns, None)) + (P(),) * 5
    return jax.shard_map(
        per_device,
        mesh=fine,
        in_specs=placed,
        out_specs=(P(rows, columns, None), P(rows, columns, None)),
        check_vma=False,
    )
```

```python
import functools

import jax
import jax.numpy as jnp
from jax import lax
from jax.experimental import pallas as pl
from jax.experimental.pallas import tpu as pltpu
from jax.sharding import Mesh
from jax.sharding import PartitionSpec as P


F32 = jnp.float32
BF16 = jnp.bfloat16
HEADS, DIM = 8, 32
GROUPS, CHIPS, ROWS = 4, 32, 16
SENT = GROUPS * CHIPS
EPSILON = 1e-5
VMEM_LIMIT = 40 * 2**20


def iota(shape, dim):
    return lax.broadcasted_iota(jnp.int32, shape, dim)


def one_hot(condition):
    return jnp.where(condition, 1.0, 0.0).astype(BF16)


def dot(a, b):
    return jnp.dot(a, b, preferred_element_type=F32)


def dot_nt(a, b):
    return lax.dot_general(a, b, (((1,), (1,)), ((), ())), preferred_element_type=F32)


def dot_tn(a, b):
    return lax.dot_general(a, b, (((0,), (0,)), ((), ())), preferred_element_type=F32)


def standardized(*parts):
    count = sum(p.shape[-1] for p in parts)
    average = jnp.sum(sum(parts[1:], parts[0]), axis=-1, keepdims=True) * (1.0 / count)
    centered = [p - average for p in parts]
    squares = [d * d for d in centered]
    variance = jnp.sum(sum(squares[1:], squares[0]), axis=-1, keepdims=True) * (1.0 / count)
    scale = lax.rsqrt(variance + EPSILON)
    return [d * scale for d in centered]


def pack_kernel(
    x_hbm,
    mask_hbm,
    pair_hbm,
    weight_hbm,
    resolved_hbm,
    out_ref,
    resolved_out,
    x_ref,
    mask_ref,
    pair_ref,
    weight_ref,
    resolved_ref,
    message,
    pair_rows,
    arrived,
):
    copies = [
        pltpu.make_async_copy(source, to, arrived.at[n])
        for n, (source, to) in enumerate(
            [
                (pair_hbm, pair_ref),
                (weight_hbm, weight_ref),
                (x_hbm, x_ref),
                (mask_hbm, mask_ref),
                (resolved_hbm, resolved_ref),
            ]
        )
    ]
    for copy in copies:
        copy.start()
    for copy in copies:
        copy.wait()
    (normed,) = standardized(pair_ref[...].astype(F32))
    for i in range(pair_ref.shape[0]):
        pair_rows[4 * i : 4 * i + 4, :] = normed[i]
    spread = one_hot(iota((HEADS, 128), 0) == (iota((HEADS, 128), 1) // 8) % 8)
    weight = dot_tn(weight_ref[...], spread).astype(BF16)
    bias = dot(pair_rows[...].astype(BF16), weight)
    row, lane = iota((256, 128), 0), iota((256, 128), 1)
    own = (row // 32 == lane % 8) & ((row // 16) % 2 == lane // 64)
    bias = jnp.sum(jnp.where(own, bias, 0.0).reshape(16, 16, 128), axis=0)

    x = x_ref[...].astype(F32)
    message[:, 0:4, :] = x[:, :, :128]
    message[:, 8:12, :] = x[:, :, 128:]
    mask = dot(mask_ref[...].astype(F32).astype(BF16), one_hot(iota((32, 128), 0) == iota((32, 128), 1) % 32))
    mask = jnp.sum(jnp.where(iota((4, 128), 0) == iota((4, 128), 1) // 32, mask, 0.0), axis=0, keepdims=True)
    flat = message.reshape(CHIPS * ROWS, 128)
    flat[pl.ds(12, CHIPS, stride=ROWS), :] = jnp.broadcast_to(mask, (CHIPS, 128))
    resolved_out[...] = resolved_ref[...]
    for g in range(GROUPS):
        message[:, 4:8, :] = jnp.broadcast_to(bias[4 * g : 4 * g + 4][None], (CHIPS, 4, 128))
        out_ref[g * CHIPS : (g + 1) * CHIPS] = message[:, 0:13, :].astype(BF16)


def keys_of(ref, wide, weight_ref, k, c):
    low = iota((16, 8, 128), 1) < 4
    lane = iota((128, 128), 1)

    def first_halves(tiles):
        return jnp.where(low, tiles[:16], pltpu.roll(tiles[16:], 4, 1)).reshape(128, 128)

    def second_halves(tiles):
        return jnp.where(low, pltpu.roll(tiles[:16], 4, 1), tiles[16:]).reshape(128, 128)

    flat = wide.reshape(SENT * ROWS, 128)
    normed, masks, biases = [], [], []
    for s in range(GROUPS):
        mine = slice(s * CHIPS, (s + 1) * CHIPS)
        wide[mine, 0:13, :] = ref[mine].astype(F32)
        tiles = wide[mine, 0:8, :]
        x0, x1 = first_halves(tiles), first_halves(wide[mine, 8:16, :])
        normed.append(jnp.concatenate(standardized(x0, x1), axis=1).astype(BF16))
        masks.append(flat[pl.ds(s * CHIPS * ROWS + 12, CHIPS, stride=ROWS), :])
        bias = second_halves(tiles)
        biases.append(jnp.where(c == 0, bias, pltpu.roll(bias, 64, 1)))
    key_value = dot(jnp.concatenate(normed, axis=0), weight_ref[:, 256:768]).astype(BF16)
    bias = jnp.concatenate(
        [
            jnp.where(lane < 64, biases[2 * n], pltpu.roll(biases[2 * n + 1], 64, 1)).T
            for n in range(2)
        ],
        axis=0,
    )
    masks = jnp.concatenate(masks, axis=0).astype(BF16)
    spread = dot(masks, one_hot(iota((128, 128), 0) == 32 * (lane % 4) + k)).reshape(GROUPS, CHIPS, 128)
    chip, key = iota((GROUPS, CHIPS, 128), 1), iota((GROUPS, CHIPS, 128), 2)
    rows = jnp.sum(jnp.where(chip == key // 8 + 16 * ((key // 4) % 2), spread, 0.0), axis=1)
    return key_value, bias, rows, masks


def left_masks(masks, g):
    tiles = masks.astype(F32).reshape(GROUPS, 4, 8, 128)
    rows = jnp.where(g < 2, jnp.where(g == 0, tiles[:, 0], tiles[:, 1]), jnp.where(g == 2, tiles[:, 2], tiles[:, 3]))
    row = jnp.concatenate([rows[s] for s in range(GROUPS)], axis=1)
    place_of = iota((8, 512), 1) // 32 % 4
    return jnp.concatenate([jnp.where(place_of == t, row, 0.0) for t in range(4)], axis=0).astype(BF16)


def heads():
    return jnp.where(iota((HEADS, 8, 256), 2) // DIM == iota((HEADS, 8, 256), 0), 1.0, 0.0)


def first_kernel(
    place,
    own_ref,
    weight_ref,
    sides_ref,
    resolved_ref,
    value_ref,
    query_ref,
    score_ref,
    gate_ref,
    residual_ref,
    present_ref,
    wide_sides_ref,
    right_mask_ref,
    pair_mask_ref,
    count_ref,
    wide,
):
    g, k, c = place()
    key_value, bias, key_masks, masks = keys_of(own_ref, wide, weight_ref, k, c)
    value_ref[...] = key_value[:, 256:]
    flat = wide.reshape(SENT * ROWS, 128)
    x0, x1 = (
        jnp.concatenate(
            [flat[pl.ds(s * CHIPS * ROWS + row + g, CHIPS, stride=ROWS), :] for s in range(GROUPS)], axis=0
        )
        for row in (0, 8)
    )
    residual_ref[...] = jnp.concatenate([x0, x1], axis=1)
    normed = jnp.concatenate(standardized(x0, x1), axis=1).astype(BF16)
    queries = (dot(normed, weight_ref[:, :256]) * DIM**-0.5).astype(BF16).astype(F32)
    of_head = heads()
    for s in range(GROUPS):
        spread = queries[s * CHIPS : (s + 1) * CHIPS].reshape(GROUPS, 1, 8, 256) * of_head[None]
        spread = spread.reshape(256, 256).astype(BF16)
        query_ref[s] = spread
        score_ref[s] = dot_nt(spread, key_value[s * 128 : (s + 1) * 128, :256]) + bias + (key_masks[s : s + 1] - 1.0) * 1e9
    gate_ref[...] = jax.nn.sigmoid(dot(normed, weight_ref[:, 768:]))
    present_ref[...] = dot(masks, one_hot(iota((128, 128), 0) == 32 * g + k))
    row, lane = iota((128, 128), 0), iota((128, 128), 1)
    copied = one_hot(row % 32 == lane % 32)
    for s in range(GROUPS):
        mine = masks[s * CHIPS : (s + 1) * CHIPS].astype(F32)
        mine = jnp.sum(jnp.where(iota((CHIPS, 128), 0) == k, mine, 0.0), axis=0, keepdims=True)
        mine = jnp.where(row // 32 == lane // 32, jnp.broadcast_to(mine, (128, 128)), 0.0).astype(BF16)
        right_mask_ref[:, 128 * s : 128 * s + 128] = dot(mine, copied).astype(BF16)
    count_ref[...] = dot_nt(left_masks(masks, g), right_mask_ref[...])

    entry, place_of = iota((64, 256), 0), iota((64, 256), 1)
    four_times = one_hot(entry == (place_of // 128) * 32 + place_of % 32)
    wide_sides_ref[...] = dot_tn(sides_ref[...], four_times).astype(BF16)
    row, column = iota((256, 256), 0), iota((256, 256), 1)
    resolved = jnp.broadcast_to(resolved_ref[...].astype(F32), (128, 256)).astype(BF16)
    row_mask = dot_nt(one_hot(column == 64 * g + row // 4), resolved)
    pair_mask_ref[...] = row_mask * dot_nt(one_hot(column == 8 * k + 4 * c + row % 4), resolved)


def attend_kernel(
    place,
    other_ref,
    value_ref,
    query_ref,
    score_ref,
    gate_ref,
    residual_ref,
    present_ref,
    wide_sides_ref,
    right_mask_ref,
    weight_ref,
    final_ref,
    out_ref,
    count_ref,
    wide,
    message,
):
    g, k, c = place()
    lane = iota((128, 128), 1)
    key_value, bias, key_masks, masks = keys_of(other_ref, wide, weight_ref, k, c)
    count_ref[...] = dot_nt(left_masks(masks, g), right_mask_ref[...])
    of_head = heads()
    gated = []
    for s in range(GROUPS):
        mine, half = slice(s * CHIPS, (s + 1) * CHIPS), slice(s * 128, (s + 1) * 128)
        values = jnp.concatenate([value_ref[half, :], key_value[half, 256:]], axis=0)
        scores = dot_nt(query_ref[s], key_value[half, :256]) + bias + (key_masks[s : s + 1] - 1.0) * 1e9
        scores = jnp.concatenate([score_ref[s], scores], axis=1)
        exponent = jnp.exp(scores - jnp.max(scores, axis=-1, keepdims=True))
        weights = (exponent * (1.0 / jnp.sum(exponent, axis=-1, keepdims=True))).astype(BF16)
        mixed = dot(weights, values).reshape(GROUPS, HEADS, 8, 256) * of_head[None]
        attended = jnp.sum(mixed, axis=1).reshape(CHIPS, 256).astype(BF16)
        gated.append((gate_ref[mine, :] * attended.astype(F32)).astype(BF16))
    present = present_ref[...]

    result = residual_ref[...] + dot(jnp.concatenate(gated, axis=0), final_ref[...])
    result = result.astype(BF16).astype(F32)
    (normed_out,) = standardized(result)
    sides = dot(normed_out.astype(BF16), wide_sides_ref[...])
    left = (sides[:, :128] * present).astype(BF16)
    right = (sides[:, 128:] * present).astype(BF16).astype(F32)

    new, old = iota((128, 128), 0), iota((128, 128), 1)
    moved = one_hot(
        old == ((new // 2) % 4) * 32 + ((new // 8) % 4) * 8 + (new % 2) * 4 + new // 32
    )
    left = jnp.where(lane // 32 == new // 32, dot(moved, left), 0.0)
    left = jnp.sum(left.reshape(4, 32, 128), axis=0)
    sequence = iota((CHIPS, 128), 1) // 32
    right_row = jnp.zeros((CHIPS, 128), F32)
    for s in range(GROUPS):
        right_row = jnp.where(sequence == s, right[s * CHIPS : (s + 1) * CHIPS], right_row)

    flat = message.reshape(CHIPS * 8, 128)
    flat[pl.ds(0, CHIPS, stride=8), :] = right_row
    flat[pl.ds(1, CHIPS, stride=8), :] = jnp.zeros((CHIPS, 128), F32)
    for n in range(GROUPS):
        to = slice(n * CHIPS, (n + 1) * CHIPS)
        for part in range(2):
            rows = left[8 * n + 4 * part : 8 * n + 4 * part + 4].astype(BF16)
            out_ref[to, part] = jnp.broadcast_to(rows[None], (CHIPS, 4, 128))
        for half in range(2):
            flat[pl.ds(2 + half, CHIPS, stride=8), :] = result[to, half * 128 : (half + 1) * 128]
        out_ref[to, 2] = message[:, 0:4, :].astype(BF16)


def outer_kernel(
    place,
    both_ref,
    pair_ref,
    mask_ref,
    own_count_ref,
    other_count_ref,
    weight_ref,
    align_hbm,
    out_ref,
    wide,
    align,
    product,
    update,
    align_ref,
    left_here,
):
    _, _, c = place()
    for part in range(3):
        wide[:, 4 * part : 4 * part + 4, :] = both_ref[:, part].astype(F32)
    flat = wide.reshape(2 * SENT * ROWS, 128)
    lane = iota((CHIPS, 128), 1)

    def row_of(core, source, row):
        return flat[pl.ds((core * SENT + source * CHIPS) * ROWS + row, CHIPS, stride=ROWS), :]

    for t in range(GROUPS):
        for half in range(2):
            align[pl.ds(half * 128 + t, CHIPS, stride=4), :] = row_of(c, t, 10 + half)
    for s in range(CHIPS):
        for half in range(2):
            rows = align[half * 128 + 4 * s : half * 128 + 4 * s + 4, :]
            align_ref[s, :, half * 128 : (half + 1) * 128] = rows.astype(BF16)
    copy = pltpu.make_async_copy(align_ref, align_hbm, left_here)
    copy.start()

    rights = [row_of(c, t, 8) for t in range(GROUPS)]
    right = []
    for s in range(GROUPS):
        tile = rights[s]
        for t in range(GROUPS):
            if t != s:
                tile = jnp.where(lane // 32 == t, pltpu.roll(rights[t], (32 * (t - s)) % 128, 1), tile)
        right.append(tile)
    right = jnp.concatenate(right, axis=0)
    own_counts, other_counts = own_count_ref[...], other_count_ref[...]
    counts = [jnp.where(c == o, own_counts, other_counts) for o in range(2)]

    right = right.astype(BF16)
    for o in range(2):
        for t in range(GROUPS):
            for half in range(2):
                slab = (o * GROUPS + t) * 2 + half
                left = jnp.concatenate([row_of(o, t, 2 * s + half) for s in range(GROUPS)], axis=0).astype(BF16)
                product[slab * 128 : (slab + 1) * 128, :] = dot_tn(left, right)

    block = iota((64, 128), 1) // 32
    total = jnp.zeros((256, 128), F32)
    for n in range(8):
        given = [product[pl.ds(4 * n + m, 64, stride=32), :] for m in range(4)]
        turned = []
        for j in range(4):
            tile = given[j]
            for m in range(4):
                if m != j:
                    tile = jnp.where(block == m, pltpu.roll(given[m], (32 * (m - j)) % 128, 1), tile)
            turned.append(tile.astype(BF16))
        total = total + dot(jnp.concatenate(turned, axis=0), weight_ref[n * 128 : (n + 1) * 128, :])

    for o in range(2):
        for t in range(GROUPS):
            first = (o * GROUPS + t) * 8
            for j in range(4):
                value = total[j * 64 + first : j * 64 + first + 8] / counts[o][8 * t : 8 * t + 8, 32 * j : 32 * j + 1]
                update[pl.ds((4 * o + t) * 4 + j, 8, stride=32), :] = value

    update[...] = mask_ref[...] * update[...]
    for i in range(64):
        out_ref[i] = (pair_ref[i].astype(F32) + update[4 * i : 4 * i + 4, :]).astype(BF16)
    copy.wait()


def call(kernel, shapes, scratch, flops, size, interpret, **more):
    return pl.pallas_call(
        kernel,
        out_shape=shapes,
        scratch_shapes=scratch,
        compiler_params=pltpu.CompilerParams(vmem_limit_bytes=VMEM_LIMIT),
        cost_estimate=pl.CostEstimate(flops=flops, bytes_accessed=size, transcendentals=0),
        interpret=interpret,
        **more,
    )


def pack(x, mask, pair, weight, resolved, interpret=False):
    arrays = (x, mask.T, pair, weight.T, resolved.reshape(1, 256))
    scratch = [pltpu.VMEM(a.shape, a.dtype) for a in arrays]
    scratch += [
        pltpu.VMEM((CHIPS, ROWS, 128), F32),
        pltpu.VMEM((256, 128), F32),
        pltpu.SemaphoreType.DMA((5,)),
    ]
    specs = [pl.BlockSpec(memory_space=pltpu.HBM)] * 5
    if not interpret:
        arrays = [pltpu.with_memory_space_constraint(a, pltpu.HBM) for a in arrays]
    shapes = (jax.ShapeDtypeStruct((SENT, 13, 128), BF16), jax.ShapeDtypeStruct((1, 256), jnp.int32))
    return call(pack_kernel, shapes, scratch, 10**7, 10**6, interpret, in_specs=specs)(*arrays)


def first(place, own, weight, sides, resolved, interpret=False):
    kernel = functools.partial(first_kernel, place)
    shapes = [
        jax.ShapeDtypeStruct(shape, dtype)
        for shape, dtype in [
            ((512, 256), BF16),
            ((GROUPS, 256, 256), BF16),
            ((GROUPS, 256, 128), F32),
            ((128, 256), F32),
            ((128, 256), F32),
            ((128, 128), F32),
            ((256, 256), BF16),
            ((128, 512), BF16),
            ((256, 128), F32),
            ((32, 128), F32),
        ]
    ]
    scratch = [pltpu.VMEM((SENT, ROWS, 128), F32)]
    return call(kernel, shapes, scratch, 10**9, 2 * 10**6, interpret)(
        own, weight, sides.T, resolved
    )


def attend(place, other, mine, weight, final, interpret=False):
    scratch = [pltpu.VMEM((SENT, ROWS, 128), F32), pltpu.VMEM((CHIPS, 8, 128), F32)]
    shapes = (jax.ShapeDtypeStruct((SENT, 3, 4, 128), BF16), jax.ShapeDtypeStruct((32, 128), F32))
    kernel = functools.partial(attend_kernel, place)
    return call(kernel, shapes, scratch, 10**9, 2 * 10**6, interpret)(other, *mine, weight, final)


def outer(place, both, pair, pair_mask, own_counts, other_counts, weight, interpret=False):
    scratch = [
        pltpu.VMEM((2 * SENT, ROWS, 128), F32),
        pltpu.VMEM((256, 128), F32),
        pltpu.VMEM((2048, 128), F32),
        pltpu.VMEM((256, 128), F32),
        pltpu.VMEM((CHIPS, 4, 256), BF16),
        pltpu.SemaphoreType.DMA,
    ]
    shapes = (jax.ShapeDtypeStruct((CHIPS, 4, 256), BF16), jax.ShapeDtypeStruct((64, 4, 128), BF16))
    kernel = functools.partial(outer_kernel, place)
    specs = (pl.BlockSpec(memory_space=pltpu.HBM), pl.BlockSpec(memory_space=pltpu.VMEM))
    return call(kernel, shapes, scratch, 10**9, 2 * 10**6, interpret, out_specs=specs)(
        both, pair, pair_mask, own_counts, other_counts, weight
    )


def my_place():
    return lax.axis_index("seq"), lax.axis_index("chip"), lax.axis_index("core")


def exchange(messages):
    return lax.all_to_all(messages, ("seq", "chip"), 0, 0, tiled=True)


def per_device(x, mask, resolved, pair, combined, bias_weight, final, sides, outer_weight):
    messages, resolved = pack(x, mask, pair, bias_weight, resolved)
    own = exchange(messages)
    other = lax.ppermute(own, "core", [(0, 1), (1, 0)])
    *mine, pair_mask, own_counts = first(my_place, own, combined, sides, resolved)
    messages, other_counts = attend(my_place, other, mine, combined, final)
    both = lax.all_gather(exchange(messages), "core", axis=0, tiled=True)
    return outer(my_place, both, pair, pair_mask, own_counts, other_counts, outer_weight)


def solution(mesh):
    crop, seq, res = (mesh.shape[a] for a in ("crop", "seq", "res"))
    fine = Mesh(mesh.devices.reshape(crop, seq, res // 2, 2), ("crop", "seq", "chip", "core"))
    rows, columns = ("crop", "seq"), ("chip", "core")
    placed = (P(rows, columns, None), P(rows, columns), P("crop"), P(rows, columns, None)) + (P(),) * 5
    return jax.shard_map(
        per_device,
        mesh=fine,
        in_specs=placed,
        out_specs=(P(rows, columns, None), P(rows, columns, None)),
        check_vma=False,
    )
```

```python
import functools

import jax
import jax.numpy as jnp
from jax import lax
from jax.experimental import pallas as pl
from jax.experimental.pallas import tpu as pltpu
from jax.sharding import Mesh
from jax.sharding import PartitionSpec as P


F32 = jnp.float32
BF16 = jnp.bfloat16
HEADS, DIM = 8, 32
GROUPS, CHIPS, ROWS = 4, 32, 16
SENT = GROUPS * CHIPS
EPSILON = 1e-5
VMEM_LIMIT = 40 * 2**20


def iota(shape, dim):
    return lax.broadcasted_iota(jnp.int32, shape, dim)


def one_hot(condition):
    return jnp.where(condition, 1.0, 0.0).astype(BF16)


def dot(a, b):
    return jnp.dot(a, b, preferred_element_type=F32)


def dot_nt(a, b):
    return lax.dot_general(a, b, (((1,), (1,)), ((), ())), preferred_element_type=F32)


def dot_tn(a, b):
    return lax.dot_general(a, b, (((0,), (0,)), ((), ())), preferred_element_type=F32)


def standardized(*parts):
    count = sum(p.shape[-1] for p in parts)
    average = jnp.sum(sum(parts[1:], parts[0]), axis=-1, keepdims=True) * (1.0 / count)
    centered = [p - average for p in parts]
    squares = [d * d for d in centered]
    variance = jnp.sum(sum(squares[1:], squares[0]), axis=-1, keepdims=True) * (1.0 / count)
    scale = lax.rsqrt(variance + EPSILON)
    return [d * scale for d in centered]


def pack_kernel(
    x_hbm,
    mask_hbm,
    pair_hbm,
    weight_hbm,
    resolved_hbm,
    out_ref,
    resolved_out,
    x_ref,
    mask_ref,
    pair_ref,
    weight_ref,
    resolved_ref,
    message,
    pair_rows,
    arrived,
):
    copies = [
        pltpu.make_async_copy(source, to, arrived.at[n])
        for n, (source, to) in enumerate(
            [
                (pair_hbm, pair_ref),
                (weight_hbm, weight_ref),
                (x_hbm, x_ref),
                (mask_hbm, mask_ref),
                (resolved_hbm, resolved_ref),
            ]
        )
    ]
    for copy in copies:
        copy.start()
    for copy in copies:
        copy.wait()
    (normed,) = standardized(pair_ref[...].astype(F32))
    for i in range(pair_ref.shape[0]):
        pair_rows[4 * i : 4 * i + 4, :] = normed[i]
    spread = one_hot(iota((HEADS, 128), 0) == (iota((HEADS, 128), 1) // 8) % 8)
    weight = dot_tn(weight_ref[...], spread).astype(BF16)
    bias = dot(pair_rows[...].astype(BF16), weight)
    row, lane = iota((256, 128), 0), iota((256, 128), 1)
    own = (row // 32 == lane % 8) & ((row // 16) % 2 == lane // 64)
    bias = jnp.sum(jnp.where(own, bias, 0.0).reshape(16, 16, 128), axis=0)

    x = x_ref[...].astype(F32)
    message[:, 0:4, :] = x[:, :, :128]
    message[:, 8:12, :] = x[:, :, 128:]
    mask = dot(mask_ref[...].astype(F32).astype(BF16), one_hot(iota((32, 128), 0) == iota((32, 128), 1) % 32))
    mask = jnp.sum(jnp.where(iota((4, 128), 0) == iota((4, 128), 1) // 32, mask, 0.0), axis=0, keepdims=True)
    message[:, 12:14, :] = jnp.broadcast_to(mask[None], (CHIPS, 2, 128))
    for part in (0, 1, 4, 5, 6):
        rows = message[:, 2 * part : 2 * part + 2, :].astype(BF16)
        for g in range(GROUPS):
            out_ref[g * CHIPS : (g + 1) * CHIPS, part] = rows
    resolved_out[...] = resolved_ref[...]
    for g in range(GROUPS):
        for half in range(2):
            rows = bias[4 * g + 2 * half : 4 * g + 2 * half + 2].astype(BF16)
            out_ref[g * CHIPS : (g + 1) * CHIPS, 2 + half] = jnp.broadcast_to(rows[None], (CHIPS, 2, 128))


def keys_of(ref, wide, weight_ref, k, c):
    low = iota((16, 8, 128), 1) < 4
    lane = iota((128, 128), 1)

    def first_halves(tiles):
        return jnp.where(low, tiles[:16], pltpu.roll(tiles[16:], 4, 1)).reshape(128, 128)

    def second_halves(tiles):
        return jnp.where(low, pltpu.roll(tiles[:16], 4, 1), tiles[16:]).reshape(128, 128)

    flat = wide.reshape(SENT * ROWS, 128)
    normed, masks, biases = [], [], []
    for s in range(GROUPS):
        mine = slice(s * CHIPS, (s + 1) * CHIPS)
        for part in range(7):
            wide[mine, 2 * part : 2 * part + 2, :] = ref[mine, part].astype(F32)
        tiles = wide[mine, 0:8, :]
        x0, x1 = first_halves(tiles), first_halves(wide[mine, 8:16, :])
        normed.append(jnp.concatenate(standardized(x0, x1), axis=1).astype(BF16))
        masks.append(flat[pl.ds(s * CHIPS * ROWS + 12, CHIPS, stride=ROWS), :])
        bias = second_halves(tiles)
        biases.append(jnp.where(c == 0, bias, pltpu.roll(bias, 64, 1)))
    key_value = dot(jnp.concatenate(normed, axis=0), weight_ref[:, 256:768]).astype(BF16)
    bias = jnp.concatenate(
        [
            jnp.where(lane < 64, biases[2 * n], pltpu.roll(biases[2 * n + 1], 64, 1)).T
            for n in range(2)
        ],
        axis=0,
    )
    masks = jnp.concatenate(masks, axis=0).astype(BF16)
    spread = dot(masks, one_hot(iota((128, 128), 0) == 32 * (lane % 4) + k)).reshape(GROUPS, CHIPS, 128)
    chip, key = iota((GROUPS, CHIPS, 128), 1), iota((GROUPS, CHIPS, 128), 2)
    rows = jnp.sum(jnp.where(chip == key // 8 + 16 * ((key // 4) % 2), spread, 0.0), axis=1)
    return key_value, bias, rows, masks


def left_masks(masks, g):
    tiles = masks.astype(F32).reshape(GROUPS, 4, 8, 128)
    rows = jnp.where(g < 2, jnp.where(g == 0, tiles[:, 0], tiles[:, 1]), jnp.where(g == 2, tiles[:, 2], tiles[:, 3]))
    row = jnp.concatenate([rows[s] for s in range(GROUPS)], axis=1)
    place_of = iota((8, 512), 1) // 32 % 4
    return jnp.concatenate([jnp.where(place_of == t, row, 0.0) for t in range(4)], axis=0).astype(BF16)


def heads():
    return jnp.where(iota((HEADS, 8, 256), 2) // DIM == iota((HEADS, 8, 256), 0), 1.0, 0.0)


def first_kernel(
    place,
    own_ref,
    weight_ref,
    sides_ref,
    resolved_ref,
    value_ref,
    query_ref,
    score_ref,
    gate_ref,
    residual_ref,
    present_ref,
    wide_sides_ref,
    right_mask_ref,
    pair_mask_ref,
    count_ref,
    wide,
):
    g, k, c = place()
    key_value, bias, key_masks, masks = keys_of(own_ref, wide, weight_ref, k, c)
    value_ref[...] = key_value[:, 256:]
    flat = wide.reshape(SENT * ROWS, 128)
    x0, x1 = (
        jnp.concatenate(
            [flat[pl.ds(s * CHIPS * ROWS + row + g, CHIPS, stride=ROWS), :] for s in range(GROUPS)], axis=0
        )
        for row in (0, 8)
    )
    residual_ref[...] = jnp.concatenate([x0, x1], axis=1)
    normed = jnp.concatenate(standardized(x0, x1), axis=1).astype(BF16)
    queries = (dot(normed, weight_ref[:, :256]) * DIM**-0.5).astype(BF16).astype(F32)
    of_head = heads()
    for s in range(GROUPS):
        spread = queries[s * CHIPS : (s + 1) * CHIPS].reshape(GROUPS, 1, 8, 256) * of_head[None]
        spread = spread.reshape(256, 256).astype(BF16)
        query_ref[s] = spread
        score_ref[s] = dot_nt(spread, key_value[s * 128 : (s + 1) * 128, :256]) + bias + (key_masks[s : s + 1] - 1.0) * 1e9
    gate_ref[...] = jax.nn.sigmoid(dot(normed, weight_ref[:, 768:]))
    present_ref[...] = dot(masks, one_hot(iota((128, 128), 0) == 32 * g + k))
    row, lane = iota((128, 128), 0), iota((128, 128), 1)
    copied = one_hot(row % 32 == lane % 32)
    for s in range(GROUPS):
        mine = masks[s * CHIPS : (s + 1) * CHIPS].astype(F32)
        mine = jnp.sum(jnp.where(iota((CHIPS, 128), 0) == k, mine, 0.0), axis=0, keepdims=True)
        mine = jnp.where(row // 32 == lane // 32, jnp.broadcast_to(mine, (128, 128)), 0.0).astype(BF16)
        right_mask_ref[:, 128 * s : 128 * s + 128] = dot(mine, copied).astype(BF16)
    count_ref[...] = dot_nt(left_masks(masks, g), right_mask_ref[...])

    entry, place_of = iota((64, 256), 0), iota((64, 256), 1)
    four_times = one_hot(entry == (place_of // 128) * 32 + place_of % 32)
    wide_sides_ref[...] = dot_tn(sides_ref[...], four_times).astype(BF16)
    row, column = iota((256, 256), 0), iota((256, 256), 1)
    resolved = jnp.broadcast_to(resolved_ref[...].astype(F32), (128, 256)).astype(BF16)
    row_mask = dot_nt(one_hot(column == 64 * g + row // 4), resolved)
    pair_mask_ref[...] = row_mask * dot_nt(one_hot(column == 8 * k + 4 * c + row % 4), resolved)


def attend_kernel(
    place,
    other_ref,
    value_ref,
    query_ref,
    score_ref,
    gate_ref,
    residual_ref,
    present_ref,
    wide_sides_ref,
    right_mask_ref,
    weight_ref,
    final_ref,
    out_ref,
    count_ref,
    wide,
    message,
):
    g, k, c = place()
    lane = iota((128, 128), 1)
    key_value, bias, key_masks, masks = keys_of(other_ref, wide, weight_ref, k, c)
    count_ref[...] = dot_nt(left_masks(masks, g), right_mask_ref[...])
    of_head = heads()
    gated = []
    for s in range(GROUPS):
        mine, half = slice(s * CHIPS, (s + 1) * CHIPS), slice(s * 128, (s + 1) * 128)
        values = jnp.concatenate([value_ref[half, :], key_value[half, 256:]], axis=0)
        scores = dot_nt(query_ref[s], key_value[half, :256]) + bias + (key_masks[s : s + 1] - 1.0) * 1e9
        scores = jnp.concatenate([score_ref[s], scores], axis=1)
        exponent = jnp.exp(scores - jnp.max(scores, axis=-1, keepdims=True))
        weights = (exponent * (1.0 / jnp.sum(exponent, axis=-1, keepdims=True))).astype(BF16)
        mixed = dot(weights, values).reshape(GROUPS, HEADS, 8, 256) * of_head[None]
        attended = jnp.sum(mixed, axis=1).reshape(CHIPS, 256).astype(BF16)
        gated.append((gate_ref[mine, :] * attended.astype(F32)).astype(BF16))
    present = present_ref[...]

    result = residual_ref[...] + dot(jnp.concatenate(gated, axis=0), final_ref[...])
    result = result.astype(BF16).astype(F32)
    (normed_out,) = standardized(result)
    sides = dot(normed_out.astype(BF16), wide_sides_ref[...])
    left = (sides[:, :128] * present).astype(BF16)
    right = (sides[:, 128:] * present).astype(BF16).astype(F32)

    new, old = iota((128, 128), 0), iota((128, 128), 1)
    moved = one_hot(
        old == ((new // 2) % 4) * 32 + ((new // 8) % 4) * 8 + (new % 2) * 4 + new // 32
    )
    left = jnp.where(lane // 32 == new // 32, dot(moved, left), 0.0)
    left = jnp.sum(left.reshape(4, 32, 128), axis=0)
    sequence = iota((CHIPS, 128), 1) // 32
    right_row = jnp.zeros((CHIPS, 128), F32)
    for s in range(GROUPS):
        right_row = jnp.where(sequence == s, right[s * CHIPS : (s + 1) * CHIPS], right_row)

    flat = message.reshape(CHIPS * 8, 128)
    flat[pl.ds(0, CHIPS, stride=8), :] = right_row
    flat[pl.ds(1, CHIPS, stride=8), :] = jnp.zeros((CHIPS, 128), F32)
    for n in range(GROUPS):
        to = slice(n * CHIPS, (n + 1) * CHIPS)
        for part in range(2):
            rows = left[8 * n + 4 * part : 8 * n + 4 * part + 4].astype(BF16)
            out_ref[to, part] = jnp.broadcast_to(rows[None], (CHIPS, 4, 128))
        for half in range(2):
            flat[pl.ds(2 + half, CHIPS, stride=8), :] = result[to, half * 128 : (half + 1) * 128]
        out_ref[to, 2] = message[:, 0:4, :].astype(BF16)


def outer_kernel(
    place,
    both_ref,
    pair_ref,
    mask_ref,
    own_count_ref,
    other_count_ref,
    weight_ref,
    align_hbm,
    out_ref,
    wide,
    align,
    product,
    update,
    align_ref,
    left_here,
):
    _, _, c = place()
    for part in range(3):
        wide[:, 4 * part : 4 * part + 4, :] = both_ref[:, part].astype(F32)
    flat = wide.reshape(2 * SENT * ROWS, 128)
    lane = iota((CHIPS, 128), 1)

    def row_of(core, source, row):
        return flat[pl.ds((core * SENT + source * CHIPS) * ROWS + row, CHIPS, stride=ROWS), :]

    for t in range(GROUPS):
        for half in range(2):
            align[pl.ds(half * 128 + t, CHIPS, stride=4), :] = row_of(c, t, 10 + half)
    for s in range(CHIPS):
        for half in range(2):
            rows = align[half * 128 + 4 * s : half * 128 + 4 * s + 4, :]
            align_ref[s, :, half * 128 : (half + 1) * 128] = rows.astype(BF16)
    copy = pltpu.make_async_copy(align_ref, align_hbm, left_here)
    copy.start()

    rights = [row_of(c, t, 8) for t in range(GROUPS)]
    right = []
    for s in range(GROUPS):
        tile = rights[s]
        for t in range(GROUPS):
            if t != s:
                tile = jnp.where(lane // 32 == t, pltpu.roll(rights[t], (32 * (t - s)) % 128, 1), tile)
        right.append(tile)
    right = jnp.concatenate(right, axis=0)
    own_counts, other_counts = own_count_ref[...], other_count_ref[...]
    counts = [jnp.where(c == o, own_counts, other_counts) for o in range(2)]

    right = right.astype(BF16)
    for o in range(2):
        for t in range(GROUPS):
            for half in range(2):
                slab = (o * GROUPS + t) * 2 + half
                left = jnp.concatenate([row_of(o, t, 2 * s + half) for s in range(GROUPS)], axis=0).astype(BF16)
                product[slab * 128 : (slab + 1) * 128, :] = dot_tn(left, right)

    block = iota((64, 128), 1) // 32
    total = jnp.zeros((256, 128), F32)
    for n in range(8):
        given = [product[pl.ds(4 * n + m, 64, stride=32), :] for m in range(4)]
        turned = []
        for j in range(4):
            tile = given[j]
            for m in range(4):
                if m != j:
                    tile = jnp.where(block == m, pltpu.roll(given[m], (32 * (m - j)) % 128, 1), tile)
            turned.append(tile.astype(BF16))
        total = total + dot(jnp.concatenate(turned, axis=0), weight_ref[n * 128 : (n + 1) * 128, :])

    for o in range(2):
        for t in range(GROUPS):
            first = (o * GROUPS + t) * 8
            for j in range(4):
                value = total[j * 64 + first : j * 64 + first + 8] / counts[o][8 * t : 8 * t + 8, 32 * j : 32 * j + 1]
                update[pl.ds((4 * o + t) * 4 + j, 8, stride=32), :] = value

    update[...] = mask_ref[...] * update[...]
    for i in range(64):
        out_ref[i] = (pair_ref[i].astype(F32) + update[4 * i : 4 * i + 4, :]).astype(BF16)
    copy.wait()


def call(kernel, shapes, scratch, flops, size, interpret, **more):
    return pl.pallas_call(
        kernel,
        out_shape=shapes,
        scratch_shapes=scratch,
        compiler_params=pltpu.CompilerParams(vmem_limit_bytes=VMEM_LIMIT),
        cost_estimate=pl.CostEstimate(flops=flops, bytes_accessed=size, transcendentals=0),
        interpret=interpret,
        **more,
    )


def pack(x, mask, pair, weight, resolved, interpret=False):
    arrays = (x, mask.T, pair, weight.T, resolved.reshape(1, 256))
    scratch = [pltpu.VMEM(a.shape, a.dtype) for a in arrays]
    scratch += [
        pltpu.VMEM((CHIPS, ROWS, 128), F32),
        pltpu.VMEM((256, 128), F32),
        pltpu.SemaphoreType.DMA((5,)),
    ]
    specs = [pl.BlockSpec(memory_space=pltpu.HBM)] * 5
    if not interpret:
        arrays = [pltpu.with_memory_space_constraint(a, pltpu.HBM) for a in arrays]
    shapes = (jax.ShapeDtypeStruct((SENT, 7, 2, 128), BF16), jax.ShapeDtypeStruct((1, 256), jnp.int32))
    return call(pack_kernel, shapes, scratch, 10**7, 10**6, interpret, in_specs=specs)(*arrays)


def first(place, own, weight, sides, resolved, interpret=False):
    kernel = functools.partial(first_kernel, place)
    shapes = [
        jax.ShapeDtypeStruct(shape, dtype)
        for shape, dtype in [
            ((512, 256), BF16),
            ((GROUPS, 256, 256), BF16),
            ((GROUPS, 256, 128), F32),
            ((128, 256), F32),
            ((128, 256), F32),
            ((128, 128), F32),
            ((256, 256), BF16),
            ((128, 512), BF16),
            ((256, 128), F32),
            ((32, 128), F32),
        ]
    ]
    scratch = [pltpu.VMEM((SENT, ROWS, 128), F32)]
    return call(kernel, shapes, scratch, 10**9, 2 * 10**6, interpret)(
        own, weight, sides.T, resolved
    )


def attend(place, other, mine, weight, final, interpret=False):
    scratch = [pltpu.VMEM((SENT, ROWS, 128), F32), pltpu.VMEM((CHIPS, 8, 128), F32)]
    shapes = (jax.ShapeDtypeStruct((SENT, 3, 4, 128), BF16), jax.ShapeDtypeStruct((32, 128), F32))
    kernel = functools.partial(attend_kernel, place)
    return call(kernel, shapes, scratch, 10**9, 2 * 10**6, interpret)(other, *mine, weight, final)


def outer(place, both, pair, pair_mask, own_counts, other_counts, weight, interpret=False):
    scratch = [
        pltpu.VMEM((2 * SENT, ROWS, 128), F32),
        pltpu.VMEM((256, 128), F32),
        pltpu.VMEM((2048, 128), F32),
        pltpu.VMEM((256, 128), F32),
        pltpu.VMEM((CHIPS, 4, 256), BF16),
        pltpu.SemaphoreType.DMA,
    ]
    shapes = (jax.ShapeDtypeStruct((CHIPS, 4, 256), BF16), jax.ShapeDtypeStruct((64, 4, 128), BF16))
    kernel = functools.partial(outer_kernel, place)
    specs = (pl.BlockSpec(memory_space=pltpu.HBM), pl.BlockSpec(memory_space=pltpu.VMEM))
    return call(kernel, shapes, scratch, 10**9, 2 * 10**6, interpret, out_specs=specs)(
        both, pair, pair_mask, own_counts, other_counts, weight
    )


def my_place():
    return lax.axis_index("seq"), lax.axis_index("chip"), lax.axis_index("core")


def exchange(messages):
    return lax.all_to_all(messages, ("seq", "chip"), 0, 0, tiled=True)


def per_device(x, mask, resolved, pair, combined, bias_weight, final, sides, outer_weight):
    messages, resolved = pack(x, mask, pair, bias_weight, resolved)
    own = exchange(messages)
    other = lax.ppermute(own, "core", [(0, 1), (1, 0)])
    *mine, pair_mask, own_counts = first(my_place, own, combined, sides, resolved)
    messages, other_counts = attend(my_place, other, mine, combined, final)
    both = lax.all_gather(exchange(messages), "core", axis=0, tiled=True)
    return outer(my_place, both, pair, pair_mask, own_counts, other_counts, outer_weight)


def solution(mesh):
    crop, seq, res = (mesh.shape[a] for a in ("crop", "seq", "res"))
    fine = Mesh(mesh.devices.reshape(crop, seq, res // 2, 2), ("crop", "seq", "chip", "core"))
    rows, columns = ("crop", "seq"), ("chip", "core")
    placed = (P(rows, columns, None), P(rows, columns), P("crop"), P(rows, columns, None)) + (P(),) * 5
    return jax.shard_map(
        per_device,
        mesh=fine,
        in_specs=placed,
        out_specs=(P(rows, columns, None), P(rows, columns, None)),
        check_vma=False,
    )
```

```python
import functools

import jax
import jax.numpy as jnp
from jax import lax
from jax.experimental import pallas as pl
from jax.experimental.pallas import tpu as pltpu
from jax.sharding import Mesh
from jax.sharding import PartitionSpec as P


F32 = jnp.float32
BF16 = jnp.bfloat16
HEADS, DIM = 8, 32
GROUPS, CHIPS, ROWS = 4, 32, 16
SENT = GROUPS * CHIPS
EPSILON = 1e-5
VMEM_LIMIT = 40 * 2**20


def iota(shape, dim):
    return lax.broadcasted_iota(jnp.int32, shape, dim)


def one_hot(condition):
    return jnp.where(condition, 1.0, 0.0).astype(BF16)


def dot(a, b):
    return jnp.dot(a, b, preferred_element_type=F32)


def dot_nt(a, b):
    return lax.dot_general(a, b, (((1,), (1,)), ((), ())), preferred_element_type=F32)


def dot_tn(a, b):
    return lax.dot_general(a, b, (((0,), (0,)), ((), ())), preferred_element_type=F32)


def standardized(*parts):
    count = sum(p.shape[-1] for p in parts)
    average = jnp.sum(sum(parts[1:], parts[0]), axis=-1, keepdims=True) * (1.0 / count)
    centered = [p - average for p in parts]
    squares = [d * d for d in centered]
    variance = jnp.sum(sum(squares[1:], squares[0]), axis=-1, keepdims=True) * (1.0 / count)
    scale = lax.rsqrt(variance + EPSILON)
    return [d * scale for d in centered]


def pack_kernel(
    x_hbm,
    mask_hbm,
    pair_hbm,
    weight_hbm,
    resolved_hbm,
    out_ref,
    resolved_out,
    x_ref,
    mask_ref,
    pair_ref,
    weight_ref,
    resolved_ref,
    message,
    pair_rows,
    arrived,
):
    copies = [
        pltpu.make_async_copy(source, to, arrived.at[n])
        for n, (source, to) in enumerate(
            [
                (pair_hbm, pair_ref),
                (weight_hbm, weight_ref),
                (x_hbm, x_ref),
                (mask_hbm, mask_ref),
                (resolved_hbm, resolved_ref),
            ]
        )
    ]
    for copy in copies:
        copy.start()
    for copy in copies:
        copy.wait()
    (normed,) = standardized(pair_ref[...].astype(F32))
    for i in range(pair_ref.shape[0]):
        pair_rows[4 * i : 4 * i + 4, :] = normed[i]
    spread = one_hot(iota((HEADS, 128), 0) == (iota((HEADS, 128), 1) // 8) % 8)
    weight = dot_tn(weight_ref[...], spread).astype(BF16)
    bias = dot(pair_rows[...].astype(BF16), weight)
    row, lane = iota((256, 128), 0), iota((256, 128), 1)
    own = (row // 32 == lane % 8) & ((row // 16) % 2 == lane // 64)
    bias = jnp.sum(jnp.where(own, bias, 0.0).reshape(16, 16, 128), axis=0)

    x = x_ref[...].astype(F32)
    message[:, 0:4, :] = x[:, :, :128]
    message[:, 8:12, :] = x[:, :, 128:]
    mask = dot(mask_ref[...].astype(F32).astype(BF16), one_hot(iota((32, 128), 0) == iota((32, 128), 1) % 32))
    mask = jnp.sum(jnp.where(iota((4, 128), 0) == iota((4, 128), 1) // 32, mask, 0.0), axis=0, keepdims=True)
    message[:, 12:14, :] = jnp.broadcast_to(mask[None], (CHIPS, 2, 128))
    for part in (0, 1, 4, 5, 6):
        rows = message[:, 2 * part : 2 * part + 2, :].astype(BF16)
        for g in range(GROUPS):
            out_ref[g * CHIPS : (g + 1) * CHIPS, part] = rows
    resolved_out[...] = resolved_ref[...]
    for g in range(GROUPS):
        for half in range(2):
            rows = bias[4 * g + 2 * half : 4 * g + 2 * half + 2].astype(BF16)
            out_ref[g * CHIPS : (g + 1) * CHIPS, 2 + half] = jnp.broadcast_to(rows[None], (CHIPS, 2, 128))


def keys_of(ref, wide, weight_ref, k, c):
    low = iota((16, 8, 128), 1) < 4
    lane = iota((128, 128), 1)

    def first_halves(tiles):
        return jnp.where(low, tiles[:16], pltpu.roll(tiles[16:], 4, 1)).reshape(128, 128)

    def second_halves(tiles):
        return jnp.where(low, pltpu.roll(tiles[:16], 4, 1), tiles[16:]).reshape(128, 128)

    flat = wide.reshape(SENT * ROWS, 128)
    normed, masks, biases = [], [], []
    for s in range(GROUPS):
        mine = slice(s * CHIPS, (s + 1) * CHIPS)
        for part in range(7):
            wide[mine, 2 * part : 2 * part + 2, :] = ref[mine, part].astype(F32)
        tiles = wide[mine, 0:8, :]
        x0, x1 = first_halves(tiles), first_halves(wide[mine, 8:16, :])
        normed.append(jnp.concatenate(standardized(x0, x1), axis=1).astype(BF16))
        masks.append(flat[pl.ds(s * CHIPS * ROWS + 12, CHIPS, stride=ROWS), :])
        bias = second_halves(tiles)
        biases.append(jnp.where(c == 0, bias, pltpu.roll(bias, 64, 1)))
    key_value = dot(jnp.concatenate(normed, axis=0), weight_ref[:, 256:768]).astype(BF16)
    bias = jnp.concatenate(
        [
            jnp.where(lane < 64, biases[2 * n], pltpu.roll(biases[2 * n + 1], 64, 1)).T
            for n in range(2)
        ],
        axis=0,
    )
    masks = jnp.concatenate(masks, axis=0).astype(BF16)
    spread = dot(masks, one_hot(iota((128, 128), 0) == 32 * (lane % 4) + k)).reshape(GROUPS, CHIPS, 128)
    chip, key = iota((GROUPS, CHIPS, 128), 1), iota((GROUPS, CHIPS, 128), 2)
    rows = jnp.sum(jnp.where(chip == key // 8 + 16 * ((key // 4) % 2), spread, 0.0), axis=1)
    return key_value, bias, rows, masks


def left_masks(masks, g):
    tiles = masks.astype(F32).reshape(GROUPS, 4, 8, 128)
    rows = jnp.where(g < 2, jnp.where(g == 0, tiles[:, 0], tiles[:, 1]), jnp.where(g == 2, tiles[:, 2], tiles[:, 3]))
    row = jnp.concatenate([rows[s] for s in range(GROUPS)], axis=1)
    place_of = iota((8, 512), 1) // 32 % 4
    return jnp.concatenate([jnp.where(place_of == t, row, 0.0) for t in range(4)], axis=0).astype(BF16)


def heads():
    return jnp.where(iota((HEADS, 8, 256), 2) // DIM == iota((HEADS, 8, 256), 0), 1.0, 0.0)


def first_kernel(
    place,
    own_ref,
    weight_ref,
    sides_ref,
    resolved_ref,
    value_ref,
    query_ref,
    score_ref,
    gate_ref,
    residual_ref,
    present_ref,
    wide_sides_ref,
    right_mask_ref,
    pair_mask_ref,
    count_ref,
    wide,
):
    g, k, c = place()
    key_value, bias, key_masks, masks = keys_of(own_ref, wide, weight_ref, k, c)
    value_ref[...] = key_value[:, 256:]
    flat = wide.reshape(SENT * ROWS, 128)
    x0, x1 = (
        jnp.concatenate(
            [flat[pl.ds(s * CHIPS * ROWS + row + g, CHIPS, stride=ROWS), :] for s in range(GROUPS)], axis=0
        )
        for row in (0, 8)
    )
    residual_ref[...] = jnp.concatenate([x0, x1], axis=1)
    normed = jnp.concatenate(standardized(x0, x1), axis=1).astype(BF16)
    queries = (dot(normed, weight_ref[:, :256]) * DIM**-0.5).astype(BF16).astype(F32)
    of_head = heads()
    for s in range(GROUPS):
        spread = queries[s * CHIPS : (s + 1) * CHIPS].reshape(GROUPS, 1, 8, 256) * of_head[None]
        spread = spread.reshape(256, 256).astype(BF16)
        query_ref[s] = spread
        score_ref[s] = dot_nt(spread, key_value[s * 128 : (s + 1) * 128, :256]) + bias + (key_masks[s : s + 1] - 1.0) * 1e9
    gate_ref[...] = jax.nn.sigmoid(dot(normed, weight_ref[:, 768:]))
    present_ref[...] = dot(masks, one_hot(iota((128, 128), 0) == 32 * g + k))
    row, lane = iota((128, 128), 0), iota((128, 128), 1)
    copied = one_hot(row % 32 == lane % 32)
    for s in range(GROUPS):
        mine = masks[s * CHIPS : (s + 1) * CHIPS].astype(F32)
        mine = jnp.sum(jnp.where(iota((CHIPS, 128), 0) == k, mine, 0.0), axis=0, keepdims=True)
        mine = jnp.where(row // 32 == lane // 32, jnp.broadcast_to(mine, (128, 128)), 0.0).astype(BF16)
        right_mask_ref[:, 128 * s : 128 * s + 128] = dot(mine, copied).astype(BF16)
    count_ref[...] = dot_nt(left_masks(masks, g), right_mask_ref[...])

    entry, place_of = iota((64, 384), 0), iota((64, 384), 1)
    copies = one_hot(entry == jnp.where(place_of < 256, place_of // 8, 32 + place_of % 32))
    wide_sides_ref[...] = dot_tn(sides_ref[...], copies).astype(BF16)
    row, column = iota((256, 256), 0), iota((256, 256), 1)
    resolved = jnp.broadcast_to(resolved_ref[...].astype(F32), (128, 256)).astype(BF16)
    row_mask = dot_nt(one_hot(column == 64 * g + row // 4), resolved)
    pair_mask_ref[...] = row_mask * dot_nt(one_hot(column == 8 * k + 4 * c + row % 4), resolved)


def attend_kernel(
    place,
    other_ref,
    value_ref,
    query_ref,
    score_ref,
    gate_ref,
    residual_ref,
    present_ref,
    wide_sides_ref,
    right_mask_ref,
    weight_ref,
    final_ref,
    out_ref,
    count_ref,
    wide,
    message,
):
    g, k, c = place()
    key_value, bias, key_masks, masks = keys_of(other_ref, wide, weight_ref, k, c)
    count_ref[...] = dot_nt(left_masks(masks, g), right_mask_ref[...])
    of_head = heads()
    gated = []
    for s in range(GROUPS):
        mine, half = slice(s * CHIPS, (s + 1) * CHIPS), slice(s * 128, (s + 1) * 128)
        values = jnp.concatenate([value_ref[half, :], key_value[half, 256:]], axis=0)
        scores = dot_nt(query_ref[s], key_value[half, :256]) + bias + (key_masks[s : s + 1] - 1.0) * 1e9
        scores = jnp.concatenate([score_ref[s], scores], axis=1)
        exponent = jnp.exp(scores - jnp.max(scores, axis=-1, keepdims=True))
        weights = (exponent * (1.0 / jnp.sum(exponent, axis=-1, keepdims=True))).astype(BF16)
        mixed = dot(weights, values).reshape(GROUPS, HEADS, 8, 256) * of_head[None]
        attended = jnp.sum(mixed, axis=1).reshape(CHIPS, 256).astype(BF16)
        gated.append((gate_ref[mine, :] * attended.astype(F32)).astype(BF16))
    present = present_ref[...]

    result = residual_ref[...] + dot(jnp.concatenate(gated, axis=0), final_ref[...])
    result = result.astype(BF16).astype(F32)
    (normed_out,) = standardized(result)
    sides = dot(normed_out.astype(BF16), wide_sides_ref[...])
    left = jnp.concatenate([sides[:, :128] * present, sides[:, 128:256] * present], axis=1).astype(BF16)
    right = (sides[:, 256:] * present).astype(BF16).astype(F32)

    new, old = iota((128, 128), 0), iota((128, 128), 1)
    moved = one_hot(old == (new % 4) * 32 + ((new // 4) % 4) * 8 + new // 16)
    left = jnp.where(iota((128, 256), 1) % 8 == iota((128, 256), 0) // 16, dot(moved, left), 0.0)
    left = jnp.sum(left.reshape(8, 16, 256), axis=0)
    sequence = iota((CHIPS, 128), 1) // 32
    right_row = jnp.zeros((CHIPS, 128), F32)
    for s in range(GROUPS):
        right_row = jnp.where(sequence == s, right[s * CHIPS : (s + 1) * CHIPS], right_row)

    flat = message.reshape(CHIPS * 8, 128)
    flat[pl.ds(0, CHIPS, stride=8), :] = right_row
    flat[pl.ds(1, CHIPS, stride=8), :] = jnp.zeros((CHIPS, 128), F32)
    for n in range(GROUPS):
        to = slice(n * CHIPS, (n + 1) * CHIPS)
        for part in range(2):
            rows = left[4 * n : 4 * n + 4, 128 * part : 128 * part + 128].astype(BF16)
            out_ref[to, part] = jnp.broadcast_to(rows[None], (CHIPS, 4, 128))
        for half in range(2):
            flat[pl.ds(2 + half, CHIPS, stride=8), :] = result[to, half * 128 : (half + 1) * 128]
        out_ref[to, 2] = message[:, 0:4, :].astype(BF16)


def outer_kernel(
    place,
    both_ref,
    pair_ref,
    mask_ref,
    own_count_ref,
    other_count_ref,
    weight_ref,
    align_hbm,
    out_ref,
    wide,
    align,
    product,
    update,
    align_ref,
    left_here,
):
    _, _, c = place()
    for part in range(3):
        wide[:, 4 * part : 4 * part + 4, :] = both_ref[:, part].astype(F32)
    flat = wide.reshape(2 * SENT * ROWS, 128)
    lane = iota((CHIPS, 128), 1)

    def row_of(core, source, row):
        return flat[pl.ds((core * SENT + source * CHIPS) * ROWS + row, CHIPS, stride=ROWS), :]

    for t in range(GROUPS):
        for half in range(2):
            align[pl.ds(half * 128 + t, CHIPS, stride=4), :] = row_of(c, t, 10 + half)
    for s in range(CHIPS):
        for half in range(2):
            rows = align[half * 128 + 4 * s : half * 128 + 4 * s + 4, :]
            align_ref[s, :, half * 128 : (half + 1) * 128] = rows.astype(BF16)
    copy = pltpu.make_async_copy(align_ref, align_hbm, left_here)
    copy.start()

    rights = [row_of(c, t, 8) for t in range(GROUPS)]
    right = []
    for s in range(GROUPS):
        tile = rights[s]
        for t in range(GROUPS):
            if t != s:
                tile = jnp.where(lane // 32 == t, pltpu.roll(rights[t], (32 * (t - s)) % 128, 1), tile)
        right.append(tile)
    right = jnp.concatenate(right, axis=0)
    own_counts, other_counts = own_count_ref[...], other_count_ref[...]
    counts = [jnp.where(c == o, own_counts, other_counts) for o in range(2)]

    right = right.astype(BF16)
    lefts = [
        jnp.concatenate([row_of(o, t, 4 * part + s) for s in range(GROUPS)], axis=0).astype(BF16)
        for o in range(2)
        for t in range(GROUPS)
        for part in range(2)
    ]
    product[...] = dot_tn(jnp.concatenate(lefts, axis=1), right)

    block = iota((64, 128), 1) // 32
    columns = []
    for n in range(8):
        given = [
            jnp.concatenate([product[256 * i + 8 * m : 256 * i + 8 * m + 8, :] for i in range(8)], axis=0)
            for m in range(4 * n, 4 * n + 4)
        ]
        turned = []
        for j in range(4):
            tile = given[j]
            for m in range(4):
                if m != j:
                    tile = jnp.where(block == m, pltpu.roll(given[m], (32 * (m - j)) % 128, 1), tile)
            turned.append(tile.astype(BF16))
        columns.append(jnp.concatenate(turned, axis=0))
    total = dot(jnp.concatenate(columns, axis=1), weight_ref[...])

    for o in range(2):
        for t in range(GROUPS):
            first = (o * GROUPS + t) * 8
            for j in range(4):
                value = total[j * 64 + first : j * 64 + first + 8] / counts[o][8 * t : 8 * t + 8, 32 * j : 32 * j + 1]
                update[pl.ds((4 * o + t) * 4 + j, 8, stride=32), :] = value

    update[...] = mask_ref[...] * update[...]
    for i in range(64):
        out_ref[i] = (pair_ref[i].astype(F32) + update[4 * i : 4 * i + 4, :]).astype(BF16)
    copy.wait()


def call(kernel, shapes, scratch, flops, size, interpret, **more):
    return pl.pallas_call(
        kernel,
        out_shape=shapes,
        scratch_shapes=scratch,
        compiler_params=pltpu.CompilerParams(vmem_limit_bytes=VMEM_LIMIT),
        cost_estimate=pl.CostEstimate(flops=flops, bytes_accessed=size, transcendentals=0),
        interpret=interpret,
        **more,
    )


def pack(x, mask, pair, weight, resolved, interpret=False):
    arrays = (x, mask.T, pair, weight.T, resolved.reshape(1, 256))
    scratch = [pltpu.VMEM(a.shape, a.dtype) for a in arrays]
    scratch += [
        pltpu.VMEM((CHIPS, ROWS, 128), F32),
        pltpu.VMEM((256, 128), F32),
        pltpu.SemaphoreType.DMA((5,)),
    ]
    specs = [pl.BlockSpec(memory_space=pltpu.HBM)] * 5
    if not interpret:
        arrays = [pltpu.with_memory_space_constraint(a, pltpu.HBM) for a in arrays]
    shapes = (jax.ShapeDtypeStruct((SENT, 7, 2, 128), BF16), jax.ShapeDtypeStruct((1, 256), jnp.int32))
    return call(pack_kernel, shapes, scratch, 10**7, 10**6, interpret, in_specs=specs)(*arrays)


def first(place, own, weight, sides, resolved, interpret=False):
    kernel = functools.partial(first_kernel, place)
    shapes = [
        jax.ShapeDtypeStruct(shape, dtype)
        for shape, dtype in [
            ((512, 256), BF16),
            ((GROUPS, 256, 256), BF16),
            ((GROUPS, 256, 128), F32),
            ((128, 256), F32),
            ((128, 256), F32),
            ((128, 128), F32),
            ((256, 384), BF16),
            ((128, 512), BF16),
            ((256, 128), F32),
            ((32, 128), F32),
        ]
    ]
    scratch = [pltpu.VMEM((SENT, ROWS, 128), F32)]
    return call(kernel, shapes, scratch, 10**9, 2 * 10**6, interpret)(
        own, weight, sides.T, resolved
    )


def attend(place, other, mine, weight, final, interpret=False):
    scratch = [pltpu.VMEM((SENT, ROWS, 128), F32), pltpu.VMEM((CHIPS, 8, 128), F32)]
    shapes = (jax.ShapeDtypeStruct((SENT, 3, 4, 128), BF16), jax.ShapeDtypeStruct((32, 128), F32))
    kernel = functools.partial(attend_kernel, place)
    return call(kernel, shapes, scratch, 10**9, 2 * 10**6, interpret)(other, *mine, weight, final)


def outer(place, both, pair, pair_mask, own_counts, other_counts, weight, interpret=False):
    scratch = [
        pltpu.VMEM((2 * SENT, ROWS, 128), F32),
        pltpu.VMEM((256, 128), F32),
        pltpu.VMEM((2048, 128), F32),
        pltpu.VMEM((256, 128), F32),
        pltpu.VMEM((CHIPS, 4, 256), BF16),
        pltpu.SemaphoreType.DMA,
    ]
    shapes = (jax.ShapeDtypeStruct((CHIPS, 4, 256), BF16), jax.ShapeDtypeStruct((64, 4, 128), BF16))
    kernel = functools.partial(outer_kernel, place)
    specs = (pl.BlockSpec(memory_space=pltpu.HBM), pl.BlockSpec(memory_space=pltpu.VMEM))
    return call(kernel, shapes, scratch, 10**9, 2 * 10**6, interpret, out_specs=specs)(
        both, pair, pair_mask, own_counts, other_counts, weight
    )


def my_place():
    return lax.axis_index("seq"), lax.axis_index("chip"), lax.axis_index("core")


def exchange(messages):
    return lax.all_to_all(messages, ("seq", "chip"), 0, 0, tiled=True)


def per_device(x, mask, resolved, pair, combined, bias_weight, final, sides, outer_weight):
    messages, resolved = pack(x, mask, pair, bias_weight, resolved)
    own = exchange(messages)
    other = lax.ppermute(own, "core", [(0, 1), (1, 0)])
    *mine, pair_mask, own_counts = first(my_place, own, combined, sides, resolved)
    messages, other_counts = attend(my_place, other, mine, combined, final)
    both = lax.all_gather(exchange(messages), "core", axis=0, tiled=True)
    return outer(my_place, both, pair, pair_mask, own_counts, other_counts, outer_weight)


def solution(mesh):
    crop, seq, res = (mesh.shape[a] for a in ("crop", "seq", "res"))
    fine = Mesh(mesh.devices.reshape(crop, seq, res // 2, 2), ("crop", "seq", "chip", "core"))
    rows, columns = ("crop", "seq"), ("chip", "core")
    placed = (P(rows, columns, None), P(rows, columns), P("crop"), P(rows, columns, None)) + (P(),) * 5
    return jax.shard_map(
        per_device,
        mesh=fine,
        in_specs=placed,
        out_specs=(P(rows, columns, None), P(rows, columns, None)),
        check_vma=False,
    )
```

```python
import functools

import jax
import jax.numpy as jnp
from jax import lax
from jax.experimental import pallas as pl
from jax.experimental.pallas import tpu as pltpu
from jax.sharding import Mesh
from jax.sharding import PartitionSpec as P


F32 = jnp.float32
BF16 = jnp.bfloat16
HEADS, DIM = 8, 32
GROUPS, CHIPS, ROWS = 4, 32, 16
SENT = GROUPS * CHIPS
EPSILON = 1e-5
VMEM_LIMIT = 40 * 2**20


def iota(shape, dim):
    return lax.broadcasted_iota(jnp.int32, shape, dim)


def one_hot(condition):
    return jnp.where(condition, 1.0, 0.0).astype(BF16)


def dot(a, b):
    return jnp.dot(a, b, preferred_element_type=F32)


def dot_nt(a, b):
    return lax.dot_general(a, b, (((1,), (1,)), ((), ())), preferred_element_type=F32)


def dot_tn(a, b):
    return lax.dot_general(a, b, (((0,), (0,)), ((), ())), preferred_element_type=F32)


def standardized(*parts):
    count = sum(p.shape[-1] for p in parts)
    average = jnp.sum(sum(parts[1:], parts[0]), axis=-1, keepdims=True) * (1.0 / count)
    centered = [p - average for p in parts]
    squares = [d * d for d in centered]
    variance = jnp.sum(sum(squares[1:], squares[0]), axis=-1, keepdims=True) * (1.0 / count)
    scale = lax.rsqrt(variance + EPSILON)
    return [d * scale for d in centered]


def pack_kernel(
    x_hbm,
    mask_hbm,
    pair_hbm,
    weight_hbm,
    resolved_hbm,
    out_ref,
    resolved_out,
    x_ref,
    mask_ref,
    pair_ref,
    weight_ref,
    resolved_ref,
    message,
    pair_rows,
    arrived,
):
    copies = [
        pltpu.make_async_copy(source, to, arrived.at[n])
        for n, (source, to) in enumerate(
            [
                (pair_hbm, pair_ref),
                (weight_hbm, weight_ref),
                (x_hbm, x_ref),
                (mask_hbm, mask_ref),
                (resolved_hbm, resolved_ref),
            ]
        )
    ]
    for copy in copies:
        copy.start()
    for copy in copies:
        copy.wait()
    (normed,) = standardized(pair_ref[...].astype(F32))
    for i in range(pair_ref.shape[0]):
        pair_rows[4 * i : 4 * i + 4, :] = normed[i]
    spread = one_hot(iota((HEADS, 128), 0) == (iota((HEADS, 128), 1) // 8) % 8)
    weight = dot_tn(weight_ref[...], spread).astype(BF16)
    bias = dot(pair_rows[...].astype(BF16), weight)
    row, lane = iota((256, 128), 0), iota((256, 128), 1)
    own = (row // 32 == lane % 8) & ((row // 16) % 2 == lane // 64)
    bias = jnp.sum(jnp.where(own, bias, 0.0).reshape(16, 16, 128), axis=0)

    x = x_ref[...].astype(F32)
    message[:, 0:4, :] = x[:, :, :128]
    message[:, 8:12, :] = x[:, :, 128:]
    mask = dot(mask_ref[...].astype(F32).astype(BF16), one_hot(iota((32, 128), 0) == iota((32, 128), 1) % 32))
    mask = jnp.sum(jnp.where(iota((4, 128), 0) == iota((4, 128), 1) // 32, mask, 0.0), axis=0, keepdims=True)
    message[:, 12:14, :] = jnp.broadcast_to(mask[None], (CHIPS, 2, 128))
    for part in (0, 1, 4, 5, 6):
        rows = message[:, 2 * part : 2 * part + 2, :].astype(BF16)
        for g in range(GROUPS):
            out_ref[g * CHIPS : (g + 1) * CHIPS, part] = rows
    resolved_out[...] = resolved_ref[...]
    for g in range(GROUPS):
        for half in range(2):
            rows = bias[4 * g + 2 * half : 4 * g + 2 * half + 2].astype(BF16)
            out_ref[g * CHIPS : (g + 1) * CHIPS, 2 + half] = jnp.broadcast_to(rows[None], (CHIPS, 2, 128))


def keys_of(ref, wide, weight_ref, k, c):
    low = iota((16, 8, 128), 1) < 4
    lane = iota((128, 128), 1)

    def first_halves(tiles):
        return jnp.where(low, tiles[:16], pltpu.roll(tiles[16:], 4, 1)).reshape(128, 128)

    def second_halves(tiles):
        return jnp.where(low, pltpu.roll(tiles[:16], 4, 1), tiles[16:]).reshape(128, 128)

    flat = wide.reshape(SENT * ROWS, 128)
    normed, masks, biases = [], [], []
    for s in range(GROUPS):
        mine = slice(s * CHIPS, (s + 1) * CHIPS)
        for part in range(7):
            wide[mine, 2 * part : 2 * part + 2, :] = ref[mine, part].astype(F32)
        tiles = wide[mine, 0:8, :]
        x0, x1 = first_halves(tiles), first_halves(wide[mine, 8:16, :])
        normed.append(jnp.concatenate(standardized(x0, x1), axis=1).astype(BF16))
        masks.append(flat[pl.ds(s * CHIPS * ROWS + 12, CHIPS, stride=ROWS), :])
        bias = second_halves(tiles)
        biases.append(jnp.where(c == 0, bias, pltpu.roll(bias, 64, 1)))
    key_value = dot(jnp.concatenate(normed, axis=0), weight_ref[:, 256:768]).astype(BF16)
    bias = jnp.concatenate(
        [
            jnp.where(lane < 64, biases[2 * n], pltpu.roll(biases[2 * n + 1], 64, 1)).T
            for n in range(2)
        ],
        axis=0,
    )
    masks = jnp.concatenate(masks, axis=0).astype(BF16)
    spread = dot(masks, one_hot(iota((128, 128), 0) == 32 * (lane % 4) + k)).reshape(GROUPS, CHIPS, 128)
    chip, key = iota((GROUPS, CHIPS, 128), 1), iota((GROUPS, CHIPS, 128), 2)
    rows = jnp.sum(jnp.where(chip == key // 8 + 16 * ((key // 4) % 2), spread, 0.0), axis=1)
    return key_value, bias, rows, masks


def left_masks(masks, g):
    tiles = masks.astype(F32).reshape(GROUPS, 4, 8, 128)
    rows = jnp.where(g < 2, jnp.where(g == 0, tiles[:, 0], tiles[:, 1]), jnp.where(g == 2, tiles[:, 2], tiles[:, 3]))
    row = jnp.concatenate([rows[s] for s in range(GROUPS)], axis=1)
    place_of = iota((8, 512), 1) // 32 % 4
    return jnp.concatenate([jnp.where(place_of == t, row, 0.0) for t in range(4)], axis=0).astype(BF16)


def heads():
    return jnp.where(iota((HEADS, 8, 256), 2) // DIM == iota((HEADS, 8, 256), 0), 1.0, 0.0)


def first_kernel(
    place,
    own_ref,
    weight_ref,
    sides_ref,
    resolved_ref,
    value_ref,
    query_ref,
    score_ref,
    gate_ref,
    residual_ref,
    present_ref,
    wide_sides_ref,
    right_mask_ref,
    pair_mask_ref,
    count_ref,
    wide,
):
    g, k, c = place()
    key_value, bias, key_masks, masks = keys_of(own_ref, wide, weight_ref, k, c)
    value_ref[...] = key_value[:, 256:]
    flat = wide.reshape(SENT * ROWS, 128)
    x0, x1 = (
        jnp.concatenate(
            [flat[pl.ds(s * CHIPS * ROWS + row + g, CHIPS, stride=ROWS), :] for s in range(GROUPS)], axis=0
        )
        for row in (0, 8)
    )
    residual_ref[...] = jnp.concatenate([x0, x1], axis=1)
    normed = jnp.concatenate(standardized(x0, x1), axis=1).astype(BF16)
    queries = (dot(normed, weight_ref[:, :256]) * DIM**-0.5).astype(BF16).astype(F32)
    of_head = heads()
    for s in range(GROUPS):
        spread = queries[s * CHIPS : (s + 1) * CHIPS].reshape(GROUPS, 1, 8, 256) * of_head[None]
        spread = spread.reshape(256, 256).astype(BF16)
        query_ref[s] = spread
        score_ref[s] = dot_nt(spread, key_value[s * 128 : (s + 1) * 128, :256]) + bias + (key_masks[s : s + 1] - 1.0) * 1e9
    gate_ref[...] = jax.nn.sigmoid(dot(normed, weight_ref[:, 768:]))
    present_ref[...] = dot(masks, one_hot(iota((128, 128), 0) == 32 * g + k))
    row, lane = iota((128, 128), 0), iota((128, 128), 1)
    copied = one_hot(row % 32 == lane % 32)
    for s in range(GROUPS):
        mine = masks[s * CHIPS : (s + 1) * CHIPS].astype(F32)
        mine = jnp.sum(jnp.where(iota((CHIPS, 128), 0) == k, mine, 0.0), axis=0, keepdims=True)
        mine = jnp.where(row // 32 == lane // 32, jnp.broadcast_to(mine, (128, 128)), 0.0).astype(BF16)
        right_mask_ref[:, 128 * s : 128 * s + 128] = dot(mine, copied).astype(BF16)
    count_ref[...] = dot_nt(left_masks(masks, g), right_mask_ref[...])

    entry, place_of = iota((64, 384), 0), iota((64, 384), 1)
    copies = one_hot(entry == jnp.where(place_of < 256, place_of // 8, 32 + place_of % 32))
    wide_sides_ref[...] = dot_tn(sides_ref[...], copies).astype(BF16)
    row, column = iota((256, 256), 0), iota((256, 256), 1)
    resolved = jnp.broadcast_to(resolved_ref[...].astype(F32), (128, 256)).astype(BF16)
    row_mask = dot_nt(one_hot(column == 64 * g + row // 4), resolved)
    pair_mask_ref[...] = row_mask * dot_nt(one_hot(column == 8 * k + 4 * c + row % 4), resolved)


def attend_kernel(
    place,
    other_ref,
    value_ref,
    query_ref,
    score_ref,
    gate_ref,
    residual_ref,
    present_ref,
    wide_sides_ref,
    right_mask_ref,
    weight_ref,
    final_ref,
    out_ref,
    count_ref,
    wide,
    message,
):
    g, k, c = place()
    key_value, bias, key_masks, masks = keys_of(other_ref, wide, weight_ref, k, c)
    count_ref[...] = dot_nt(left_masks(masks, g), right_mask_ref[...])
    of_head = heads()
    gated = []
    for s in range(GROUPS):
        mine, half = slice(s * CHIPS, (s + 1) * CHIPS), slice(s * 128, (s + 1) * 128)
        values = jnp.concatenate([value_ref[half, :], key_value[half, 256:]], axis=0)
        scores = dot_nt(query_ref[s], key_value[half, :256]) + bias + (key_masks[s : s + 1] - 1.0) * 1e9
        scores = jnp.concatenate([score_ref[s], scores], axis=1)
        exponent = jnp.exp(scores - jnp.max(scores, axis=-1, keepdims=True))
        weights = (exponent * (1.0 / jnp.sum(exponent, axis=-1, keepdims=True))).astype(BF16)
        mixed = dot(weights, values).reshape(GROUPS, HEADS, 8, 256) * of_head[None]
        attended = jnp.sum(mixed, axis=1).reshape(CHIPS, 256).astype(BF16)
        gated.append((gate_ref[mine, :] * attended.astype(F32)).astype(BF16))
    present = present_ref[...]

    result = residual_ref[...] + dot(jnp.concatenate(gated, axis=0), final_ref[...])
    result = result.astype(BF16).astype(F32)
    (normed_out,) = standardized(result)
    sides = dot(normed_out.astype(BF16), wide_sides_ref[...])
    left = jnp.concatenate([sides[:, :128] * present, sides[:, 128:256] * present], axis=1).astype(BF16)
    right = (sides[:, 256:] * present).astype(BF16).astype(F32)

    left = jnp.where(iota((128, 256), 1) % 8 == iota((128, 256), 0) % 8, left.astype(F32), 0.0).astype(BF16)
    to, of = iota((16, 128), 0), iota((16, 128), 1)
    left = dot(one_hot(of // 8 == (to % 4) * 4 + to // 4), left)
    sequence = iota((CHIPS, 128), 1) // 32
    right_row = jnp.zeros((CHIPS, 128), F32)
    for s in range(GROUPS):
        right_row = jnp.where(sequence == s, right[s * CHIPS : (s + 1) * CHIPS], right_row)

    flat = message.reshape(CHIPS * 8, 128)
    flat[pl.ds(0, CHIPS, stride=8), :] = right_row
    flat[pl.ds(1, CHIPS, stride=8), :] = jnp.zeros((CHIPS, 128), F32)
    for n in range(GROUPS):
        to = slice(n * CHIPS, (n + 1) * CHIPS)
        for part in range(2):
            rows = left[4 * n : 4 * n + 4, 128 * part : 128 * part + 128].astype(BF16)
            out_ref[to, part] = jnp.broadcast_to(rows[None], (CHIPS, 4, 128))
        for half in range(2):
            flat[pl.ds(2 + half, CHIPS, stride=8), :] = result[to, half * 128 : (half + 1) * 128]
        out_ref[to, 2] = message[:, 0:4, :].astype(BF16)


def outer_kernel(
    place,
    both_ref,
    pair_ref,
    mask_ref,
    own_count_ref,
    other_count_ref,
    weight_ref,
    align_hbm,
    out_ref,
    wide,
    align,
    product,
    update,
    align_ref,
    left_here,
):
    _, _, c = place()
    for part in range(3):
        wide[:, 4 * part : 4 * part + 4, :] = both_ref[:, part].astype(F32)
    flat = wide.reshape(2 * SENT * ROWS, 128)
    lane = iota((CHIPS, 128), 1)

    def row_of(core, source, row):
        return flat[pl.ds((core * SENT + source * CHIPS) * ROWS + row, CHIPS, stride=ROWS), :]

    for t in range(GROUPS):
        for half in range(2):
            align[pl.ds(half * 128 + t, CHIPS, stride=4), :] = row_of(c, t, 10 + half)
    for s in range(CHIPS):
        for half in range(2):
            rows = align[half * 128 + 4 * s : half * 128 + 4 * s + 4, :]
            align_ref[s, :, half * 128 : (half + 1) * 128] = rows.astype(BF16)
    copy = pltpu.make_async_copy(align_ref, align_hbm, left_here)
    copy.start()

    rights = [row_of(c, t, 8) for t in range(GROUPS)]
    right = []
    for s in range(GROUPS):
        tile = rights[s]
        for t in range(GROUPS):
            if t != s:
                tile = jnp.where(lane // 32 == t, pltpu.roll(rights[t], (32 * (t - s)) % 128, 1), tile)
        right.append(tile)
    right = jnp.concatenate(right, axis=0)
    own_counts, other_counts = own_count_ref[...], other_count_ref[...]
    counts = [jnp.where(c == o, own_counts, other_counts) for o in range(2)]

    right = right.astype(BF16)
    lefts = [
        jnp.concatenate([row_of(o, t, 4 * part + s) for s in range(GROUPS)], axis=0).astype(BF16)
        for o in range(2)
        for t in range(GROUPS)
        for part in range(2)
    ]
    product[...] = dot_tn(jnp.concatenate(lefts, axis=1), right)

    block = iota((64, 128), 1) // 32
    columns = []
    for n in range(8):
        given = [
            jnp.concatenate([product[256 * i + 8 * m : 256 * i + 8 * m + 8, :] for i in range(8)], axis=0)
            for m in range(4 * n, 4 * n + 4)
        ]
        turned = []
        for j in range(4):
            tile = given[j]
            for m in range(4):
                if m != j:
                    tile = jnp.where(block == m, pltpu.roll(given[m], (32 * (m - j)) % 128, 1), tile)
            turned.append(tile.astype(BF16))
        columns.append(jnp.concatenate(turned, axis=0))
    total = dot(jnp.concatenate(columns, axis=1), weight_ref[...])

    for o in range(2):
        for t in range(GROUPS):
            first = (o * GROUPS + t) * 8
            for j in range(4):
                value = total[j * 64 + first : j * 64 + first + 8] / counts[o][8 * t : 8 * t + 8, 32 * j : 32 * j + 1]
                update[pl.ds((4 * o + t) * 4 + j, 8, stride=32), :] = value

    update[...] = mask_ref[...] * update[...]
    for i in range(64):
        out_ref[i] = (pair_ref[i].astype(F32) + update[4 * i : 4 * i + 4, :]).astype(BF16)
    copy.wait()


def call(kernel, shapes, scratch, flops, size, interpret, **more):
    return pl.pallas_call(
        kernel,
        out_shape=shapes,
        scratch_shapes=scratch,
        compiler_params=pltpu.CompilerParams(vmem_limit_bytes=VMEM_LIMIT),
        cost_estimate=pl.CostEstimate(flops=flops, bytes_accessed=size, transcendentals=0),
        interpret=interpret,
        **more,
    )


def pack(x, mask, pair, weight, resolved, interpret=False):
    arrays = (x, mask.T, pair, weight.T, resolved.reshape(1, 256))
    scratch = [pltpu.VMEM(a.shape, a.dtype) for a in arrays]
    scratch += [
        pltpu.VMEM((CHIPS, ROWS, 128), F32),
        pltpu.VMEM((256, 128), F32),
        pltpu.SemaphoreType.DMA((5,)),
    ]
    specs = [pl.BlockSpec(memory_space=pltpu.HBM)] * 5
    if not interpret:
        arrays = [pltpu.with_memory_space_constraint(a, pltpu.HBM) for a in arrays]
    shapes = (jax.ShapeDtypeStruct((SENT, 7, 2, 128), BF16), jax.ShapeDtypeStruct((1, 256), jnp.int32))
    return call(pack_kernel, shapes, scratch, 10**7, 10**6, interpret, in_specs=specs)(*arrays)


def first(place, own, weight, sides, resolved, interpret=False):
    kernel = functools.partial(first_kernel, place)
    shapes = [
        jax.ShapeDtypeStruct(shape, dtype)
        for shape, dtype in [
            ((512, 256), BF16),
            ((GROUPS, 256, 256), BF16),
            ((GROUPS, 256, 128), F32),
            ((128, 256), F32),
            ((128, 256), F32),
            ((128, 128), F32),
            ((256, 384), BF16),
            ((128, 512), BF16),
            ((256, 128), F32),
            ((32, 128), F32),
        ]
    ]
    scratch = [pltpu.VMEM((SENT, ROWS, 128), F32)]
    return call(kernel, shapes, scratch, 10**9, 2 * 10**6, interpret)(
        own, weight, sides.T, resolved
    )


def attend(place, other, mine, weight, final, interpret=False):
    scratch = [pltpu.VMEM((SENT, ROWS, 128), F32), pltpu.VMEM((CHIPS, 8, 128), F32)]
    shapes = (jax.ShapeDtypeStruct((SENT, 3, 4, 128), BF16), jax.ShapeDtypeStruct((32, 128), F32))
    kernel = functools.partial(attend_kernel, place)
    return call(kernel, shapes, scratch, 10**9, 2 * 10**6, interpret)(other, *mine, weight, final)


def outer(place, both, pair, pair_mask, own_counts, other_counts, weight, interpret=False):
    scratch = [
        pltpu.VMEM((2 * SENT, ROWS, 128), F32),
        pltpu.VMEM((256, 128), F32),
        pltpu.VMEM((2048, 128), F32),
        pltpu.VMEM((256, 128), F32),
        pltpu.VMEM((CHIPS, 4, 256), BF16),
        pltpu.SemaphoreType.DMA,
    ]
    shapes = (jax.ShapeDtypeStruct((CHIPS, 4, 256), BF16), jax.ShapeDtypeStruct((64, 4, 128), BF16))
    kernel = functools.partial(outer_kernel, place)
    specs = (pl.BlockSpec(memory_space=pltpu.HBM), pl.BlockSpec(memory_space=pltpu.VMEM))
    return call(kernel, shapes, scratch, 10**9, 2 * 10**6, interpret, out_specs=specs)(
        both, pair, pair_mask, own_counts, other_counts, weight
    )


def my_place():
    return lax.axis_index("seq"), lax.axis_index("chip"), lax.axis_index("core")


def exchange(messages):
    return lax.all_to_all(messages, ("seq", "chip"), 0, 0, tiled=True)


def per_device(x, mask, resolved, pair, combined, bias_weight, final, sides, outer_weight):
    messages, resolved = pack(x, mask, pair, bias_weight, resolved)
    own = exchange(messages)
    other = lax.ppermute(own, "core", [(0, 1), (1, 0)])
    *mine, pair_mask, own_counts = first(my_place, own, combined, sides, resolved)
    messages, other_counts = attend(my_place, other, mine, combined, final)
    both = lax.all_gather(exchange(messages), "core", axis=0, tiled=True)
    return outer(my_place, both, pair, pair_mask, own_counts, other_counts, outer_weight)


def solution(mesh):
    crop, seq, res = (mesh.shape[a] for a in ("crop", "seq", "res"))
    fine = Mesh(mesh.devices.reshape(crop, seq, res // 2, 2), ("crop", "seq", "chip", "core"))
    rows, columns = ("crop", "seq"), ("chip", "core")
    placed = (P(rows, columns, None), P(rows, columns), P("crop"), P(rows, columns, None)) + (P(),) * 5
    return jax.shard_map(
        per_device,
        mesh=fine,
        in_specs=placed,
        out_specs=(P(rows, columns, None), P(rows, columns, None)),
        check_vma=False,
    )
```

```python
import functools

import jax
import jax.numpy as jnp
from jax import lax
from jax.experimental import pallas as pl
from jax.experimental.pallas import tpu as pltpu
from jax.sharding import Mesh
from jax.sharding import PartitionSpec as P


F32 = jnp.float32
BF16 = jnp.bfloat16
HEADS, DIM = 8, 32
GROUPS, CHIPS, ROWS = 4, 32, 16
SENT = GROUPS * CHIPS
EPSILON = 1e-5
VMEM_LIMIT = 40 * 2**20


def iota(shape, dim):
    return lax.broadcasted_iota(jnp.int32, shape, dim)


def one_hot(condition):
    return jnp.where(condition, 1.0, 0.0).astype(BF16)


def dot(a, b):
    return jnp.dot(a, b, preferred_element_type=F32)


def dot_nt(a, b):
    return lax.dot_general(a, b, (((1,), (1,)), ((), ())), preferred_element_type=F32)


def dot_tn(a, b):
    return lax.dot_general(a, b, (((0,), (0,)), ((), ())), preferred_element_type=F32)


def standardized(*parts):
    count = sum(p.shape[-1] for p in parts)
    average = jnp.sum(sum(parts[1:], parts[0]), axis=-1, keepdims=True) * (1.0 / count)
    centered = [p - average for p in parts]
    squares = [d * d for d in centered]
    variance = jnp.sum(sum(squares[1:], squares[0]), axis=-1, keepdims=True) * (1.0 / count)
    scale = lax.rsqrt(variance + EPSILON)
    return [d * scale for d in centered]


def pack_kernel(
    x_hbm,
    mask_hbm,
    pair_hbm,
    weight_hbm,
    resolved_hbm,
    out_ref,
    resolved_out,
    x_ref,
    mask_ref,
    pair_ref,
    weight_ref,
    resolved_ref,
    message,
    pair_rows,
    arrived,
):
    copies = [
        pltpu.make_async_copy(source, to, arrived.at[n])
        for n, (source, to) in enumerate(
            [
                (pair_hbm, pair_ref),
                (weight_hbm, weight_ref),
                (x_hbm, x_ref),
                (mask_hbm, mask_ref),
                (resolved_hbm, resolved_ref),
            ]
        )
    ]
    for copy in copies:
        copy.start()
    for copy in copies[:2]:
        copy.wait()
    (normed,) = standardized(pair_ref[...].astype(F32))
    for i in range(pair_ref.shape[0]):
        pair_rows[4 * i : 4 * i + 4, :] = normed[i]
    spread = one_hot(iota((HEADS, 128), 0) == (iota((HEADS, 128), 1) // 8) % 8)
    weight = dot_tn(weight_ref[...], spread).astype(BF16)
    bias = dot(pair_rows[...].astype(BF16), weight)
    row, lane = iota((256, 128), 0), iota((256, 128), 1)
    own = (row // 32 == lane % 8) & ((row // 16) % 2 == lane // 64)
    bias = jnp.sum(jnp.where(own, bias, 0.0).reshape(16, 16, 128), axis=0)

    for copy in copies[2:]:
        copy.wait()
    x = x_ref[...].astype(F32)
    message[:, 0:4, :] = x[:, :, :128]
    message[:, 8:12, :] = x[:, :, 128:]
    mask = dot(mask_ref[...].astype(F32).astype(BF16), one_hot(iota((32, 128), 0) == iota((32, 128), 1) % 32))
    mask = jnp.sum(jnp.where(iota((4, 128), 0) == iota((4, 128), 1) // 32, mask, 0.0), axis=0, keepdims=True)
    message[:, 12:14, :] = jnp.broadcast_to(mask[None], (CHIPS, 2, 128))
    for part in (0, 1, 4, 5, 6):
        rows = message[:, 2 * part : 2 * part + 2, :].astype(BF16)
        for g in range(GROUPS):
            out_ref[g * CHIPS : (g + 1) * CHIPS, part] = rows
    resolved_out[...] = resolved_ref[...]
    for g in range(GROUPS):
        for half in range(2):
            rows = bias[4 * g + 2 * half : 4 * g + 2 * half + 2].astype(BF16)
            out_ref[g * CHIPS : (g + 1) * CHIPS, 2 + half] = jnp.broadcast_to(rows[None], (CHIPS, 2, 128))


def keys_of(ref, wide, weight_ref, k, c):
    low = iota((16, 8, 128), 1) < 4
    lane = iota((128, 128), 1)

    def first_halves(tiles):
        return jnp.where(low, tiles[:16], pltpu.roll(tiles[16:], 4, 1)).reshape(128, 128)

    def second_halves(tiles):
        return jnp.where(low, pltpu.roll(tiles[:16], 4, 1), tiles[16:]).reshape(128, 128)

    flat = wide.reshape(SENT * ROWS, 128)
    normed, masks, biases = [], [], []
    for s in range(GROUPS):
        mine = slice(s * CHIPS, (s + 1) * CHIPS)
        for part in range(7):
            wide[mine, 2 * part : 2 * part + 2, :] = ref[mine, part].astype(F32)
        tiles = wide[mine, 0:8, :]
        x0, x1 = first_halves(tiles), first_halves(wide[mine, 8:16, :])
        normed.append(jnp.concatenate(standardized(x0, x1), axis=1).astype(BF16))
        masks.append(flat[pl.ds(s * CHIPS * ROWS + 12, CHIPS, stride=ROWS), :])
        bias = second_halves(tiles)
        biases.append(jnp.where(c == 0, bias, pltpu.roll(bias, 64, 1)))
    key_value = dot(jnp.concatenate(normed, axis=0), weight_ref[:, 256:768]).astype(BF16)
    bias = jnp.concatenate(
        [
            jnp.where(lane < 64, biases[2 * n], pltpu.roll(biases[2 * n + 1], 64, 1)).T
            for n in range(2)
        ],
        axis=0,
    )
    masks = jnp.concatenate(masks, axis=0).astype(BF16)
    spread = dot(masks, one_hot(iota((128, 128), 0) == 32 * (lane % 4) + k)).reshape(GROUPS, CHIPS, 128)
    chip, key = iota((GROUPS, CHIPS, 128), 1), iota((GROUPS, CHIPS, 128), 2)
    rows = jnp.sum(jnp.where(chip == key // 8 + 16 * ((key // 4) % 2), spread, 0.0), axis=1)
    return key_value, bias, rows, masks


def left_masks(masks, g):
    tiles = masks.astype(F32).reshape(GROUPS, 4, 8, 128)
    rows = jnp.where(g < 2, jnp.where(g == 0, tiles[:, 0], tiles[:, 1]), jnp.where(g == 2, tiles[:, 2], tiles[:, 3]))
    row = jnp.concatenate([rows[s] for s in range(GROUPS)], axis=1)
    place_of = iota((8, 512), 1) // 32 % 4
    return jnp.concatenate([jnp.where(place_of == t, row, 0.0) for t in range(4)], axis=0).astype(BF16)


def heads():
    return jnp.where(iota((HEADS, 8, 256), 2) // DIM == iota((HEADS, 8, 256), 0), 1.0, 0.0)


def first_kernel(
    place,
    own_ref,
    weight_ref,
    sides_ref,
    resolved_ref,
    value_ref,
    query_ref,
    score_ref,
    gate_ref,
    residual_ref,
    present_ref,
    wide_sides_ref,
    right_mask_ref,
    pair_mask_ref,
    count_ref,
    wide,
):
    g, k, c = place()
    key_value, bias, key_masks, masks = keys_of(own_ref, wide, weight_ref, k, c)
    value_ref[...] = key_value[:, 256:]
    flat = wide.reshape(SENT * ROWS, 128)
    x0, x1 = (
        jnp.concatenate(
            [flat[pl.ds(s * CHIPS * ROWS + row + g, CHIPS, stride=ROWS), :] for s in range(GROUPS)], axis=0
        )
        for row in (0, 8)
    )
    residual_ref[...] = jnp.concatenate([x0, x1], axis=1)
    normed = jnp.concatenate(standardized(x0, x1), axis=1).astype(BF16)
    queries = (dot(normed, weight_ref[:, :256]) * DIM**-0.5).astype(BF16).astype(F32)
    of_head = heads()
    for s in range(GROUPS):
        spread = queries[s * CHIPS : (s + 1) * CHIPS].reshape(GROUPS, 1, 8, 256) * of_head[None]
        spread = spread.reshape(256, 256).astype(BF16)
        query_ref[s] = spread
        score_ref[s] = dot_nt(spread, key_value[s * 128 : (s + 1) * 128, :256]) + bias + (key_masks[s : s + 1] - 1.0) * 1e9
    gate_ref[...] = jax.nn.sigmoid(dot(normed, weight_ref[:, 768:]))
    present_ref[...] = dot(masks, one_hot(iota((128, 128), 0) == 32 * g + k))
    row, lane = iota((128, 128), 0), iota((128, 128), 1)
    copied = one_hot(row % 32 == lane % 32)
    for s in range(GROUPS):
        mine = masks[s * CHIPS : (s + 1) * CHIPS].astype(F32)
        mine = jnp.sum(jnp.where(iota((CHIPS, 128), 0) == k, mine, 0.0), axis=0, keepdims=True)
        mine = jnp.where(row // 32 == lane // 32, jnp.broadcast_to(mine, (128, 128)), 0.0).astype(BF16)
        right_mask_ref[:, 128 * s : 128 * s + 128] = dot(mine, copied).astype(BF16)
    count_ref[...] = dot_nt(left_masks(masks, g), right_mask_ref[...])

    entry, place_of = iota((64, 384), 0), iota((64, 384), 1)
    copies = one_hot(entry == jnp.where(place_of < 256, place_of // 8, 32 + place_of % 32))
    wide_sides_ref[...] = dot_tn(sides_ref[...], copies).astype(BF16)
    row, column = iota((256, 256), 0), iota((256, 256), 1)
    resolved = jnp.broadcast_to(resolved_ref[...].astype(F32), (128, 256)).astype(BF16)
    row_mask = dot_nt(one_hot(column == 64 * g + row // 4), resolved)
    pair_mask_ref[...] = row_mask * dot_nt(one_hot(column == 8 * k + 4 * c + row % 4), resolved)


def attend_kernel(
    place,
    other_ref,
    value_ref,
    query_ref,
    score_ref,
    gate_ref,
    residual_ref,
    present_ref,
    wide_sides_ref,
    right_mask_ref,
    weight_ref,
    final_ref,
    out_ref,
    count_ref,
    wide,
    message,
):
    g, k, c = place()
    key_value, bias, key_masks, masks = keys_of(other_ref, wide, weight_ref, k, c)
    count_ref[...] = dot_nt(left_masks(masks, g), right_mask_ref[...])
    of_head = heads()
    gated = []
    for s in range(GROUPS):
        mine, half = slice(s * CHIPS, (s + 1) * CHIPS), slice(s * 128, (s + 1) * 128)
        values = jnp.concatenate([value_ref[half, :], key_value[half, 256:]], axis=0)
        scores = dot_nt(query_ref[s], key_value[half, :256]) + bias + (key_masks[s : s + 1] - 1.0) * 1e9
        scores = jnp.concatenate([score_ref[s], scores], axis=1)
        exponent = jnp.exp(scores - jnp.max(scores, axis=-1, keepdims=True))
        weights = (exponent * (1.0 / jnp.sum(exponent, axis=-1, keepdims=True))).astype(BF16)
        mixed = dot(weights, values).reshape(GROUPS, HEADS, 8, 256) * of_head[None]
        attended = jnp.sum(mixed, axis=1).reshape(CHIPS, 256).astype(BF16)
        gated.append((gate_ref[mine, :] * attended.astype(F32)).astype(BF16))
    present = present_ref[...]

    result = residual_ref[...] + dot(jnp.concatenate(gated, axis=0), final_ref[...])
    result = result.astype(BF16).astype(F32)
    (normed_out,) = standardized(result)
    sides = dot(normed_out.astype(BF16), wide_sides_ref[...])
    left = jnp.concatenate([sides[:, :128] * present, sides[:, 128:256] * present], axis=1).astype(BF16)
    right = (sides[:, 256:] * present).astype(BF16).astype(F32)

    left = jnp.where(iota((128, 256), 1) % 8 == iota((128, 256), 0) % 8, left.astype(F32), 0.0).astype(BF16)
    to, of = iota((16, 128), 0), iota((16, 128), 1)
    left = dot(one_hot(of // 8 == (to % 4) * 4 + to // 4), left)
    sequence = iota((CHIPS, 128), 1) // 32
    right_row = jnp.zeros((CHIPS, 128), F32)
    for s in range(GROUPS):
        right_row = jnp.where(sequence == s, right[s * CHIPS : (s + 1) * CHIPS], right_row)

    flat = message.reshape(CHIPS * 8, 128)
    flat[pl.ds(0, CHIPS, stride=8), :] = right_row
    flat[pl.ds(1, CHIPS, stride=8), :] = jnp.zeros((CHIPS, 128), F32)
    for n in range(GROUPS):
        to = slice(n * CHIPS, (n + 1) * CHIPS)
        for part in range(2):
            rows = left[4 * n : 4 * n + 4, 128 * part : 128 * part + 128].astype(BF16)
            out_ref[to, part] = jnp.broadcast_to(rows[None], (CHIPS, 4, 128))
        for half in range(2):
            flat[pl.ds(2 + half, CHIPS, stride=8), :] = result[to, half * 128 : (half + 1) * 128]
        out_ref[to, 2] = message[:, 0:4, :].astype(BF16)


def outer_kernel(
    place,
    both_ref,
    pair_ref,
    mask_ref,
    own_count_ref,
    other_count_ref,
    weight_ref,
    align_hbm,
    out_ref,
    wide,
    align,
    product,
    update,
    align_ref,
    left_here,
):
    _, _, c = place()
    for part in range(3):
        wide[:, 4 * part : 4 * part + 4, :] = both_ref[:, part].astype(F32)
    flat = wide.reshape(2 * SENT * ROWS, 128)
    lane = iota((CHIPS, 128), 1)

    def row_of(core, source, row):
        return flat[pl.ds((core * SENT + source * CHIPS) * ROWS + row, CHIPS, stride=ROWS), :]

    for t in range(GROUPS):
        for half in range(2):
            align[pl.ds(half * 128 + t, CHIPS, stride=4), :] = row_of(c, t, 10 + half)
    for s in range(CHIPS):
        for half in range(2):
            rows = align[half * 128 + 4 * s : half * 128 + 4 * s + 4, :]
            align_ref[s, :, half * 128 : (half + 1) * 128] = rows.astype(BF16)
    copy = pltpu.make_async_copy(align_ref, align_hbm, left_here)
    copy.start()

    rights = [row_of(c, t, 8) for t in range(GROUPS)]
    right = []
    for s in range(GROUPS):
        tile = rights[s]
        for t in range(GROUPS):
            if t != s:
                tile = jnp.where(lane // 32 == t, pltpu.roll(rights[t], (32 * (t - s)) % 128, 1), tile)
        right.append(tile)
    right = jnp.concatenate(right, axis=0)
    own_counts, other_counts = own_count_ref[...], other_count_ref[...]
    counts = [jnp.where(c == o, own_counts, other_counts) for o in range(2)]

    right = right.astype(BF16)
    lefts = [
        jnp.concatenate([row_of(o, t, 4 * part + s) for s in range(GROUPS)], axis=0).astype(BF16)
        for o in range(2)
        for t in range(GROUPS)
        for part in range(2)
    ]
    product[...] = dot_tn(jnp.concatenate(lefts, axis=1), right)

    block = iota((64, 128), 1) // 32
    columns = []
    for n in range(8):
        given = [
            jnp.concatenate([product[256 * i + 8 * m : 256 * i + 8 * m + 8, :] for i in range(8)], axis=0)
            for m in range(4 * n, 4 * n + 4)
        ]
        turned = []
        for j in range(4):
            tile = given[j]
            for m in range(4):
                if m != j:
                    tile = jnp.where(block == m, pltpu.roll(given[m], (32 * (m - j)) % 128, 1), tile)
            turned.append(tile.astype(BF16))
        columns.append(jnp.concatenate(turned, axis=0))
    total = dot(jnp.concatenate(columns, axis=1), weight_ref[...])

    for o in range(2):
        for t in range(GROUPS):
            first = (o * GROUPS + t) * 8
            for j in range(4):
                value = total[j * 64 + first : j * 64 + first + 8] / counts[o][8 * t : 8 * t + 8, 32 * j : 32 * j + 1]
                update[pl.ds((4 * o + t) * 4 + j, 8, stride=32), :] = value

    update[...] = mask_ref[...] * update[...]
    for i in range(64):
        out_ref[i] = (pair_ref[i].astype(F32) + update[4 * i : 4 * i + 4, :]).astype(BF16)
    copy.wait()


def call(kernel, shapes, scratch, flops, size, interpret, **more):
    return pl.pallas_call(
        kernel,
        out_shape=shapes,
        scratch_shapes=scratch,
        compiler_params=pltpu.CompilerParams(vmem_limit_bytes=VMEM_LIMIT),
        cost_estimate=pl.CostEstimate(flops=flops, bytes_accessed=size, transcendentals=0),
        interpret=interpret,
        **more,
    )


def pack(x, mask, pair, weight, resolved, interpret=False):
    arrays = (x, mask.T, pair, weight.T, resolved.reshape(1, 256))
    scratch = [pltpu.VMEM(a.shape, a.dtype) for a in arrays]
    scratch += [
        pltpu.VMEM((CHIPS, ROWS, 128), F32),
        pltpu.VMEM((256, 128), F32),
        pltpu.SemaphoreType.DMA((5,)),
    ]
    specs = [pl.BlockSpec(memory_space=pltpu.HBM)] * 5
    if not interpret:
        arrays = [pltpu.with_memory_space_constraint(a, pltpu.HBM) for a in arrays]
    shapes = (jax.ShapeDtypeStruct((SENT, 7, 2, 128), BF16), jax.ShapeDtypeStruct((1, 256), jnp.int32))
    return call(pack_kernel, shapes, scratch, 10**7, 10**6, interpret, in_specs=specs)(*arrays)


def first(place, own, weight, sides, resolved, interpret=False):
    kernel = functools.partial(first_kernel, place)
    shapes = [
        jax.ShapeDtypeStruct(shape, dtype)
        for shape, dtype in [
            ((512, 256), BF16),
            ((GROUPS, 256, 256), BF16),
            ((GROUPS, 256, 128), F32),
            ((128, 256), F32),
            ((128, 256), F32),
            ((128, 128), F32),
            ((256, 384), BF16),
            ((128, 512), BF16),
            ((256, 128), F32),
            ((32, 128), F32),
        ]
    ]
    scratch = [pltpu.VMEM((SENT, ROWS, 128), F32)]
    return call(kernel, shapes, scratch, 10**9, 2 * 10**6, interpret)(
        own, weight, sides.T, resolved
    )


def attend(place, other, mine, weight, final, interpret=False):
    scratch = [pltpu.VMEM((SENT, ROWS, 128), F32), pltpu.VMEM((CHIPS, 8, 128), F32)]
    shapes = (jax.ShapeDtypeStruct((SENT, 3, 4, 128), BF16), jax.ShapeDtypeStruct((32, 128), F32))
    kernel = functools.partial(attend_kernel, place)
    return call(kernel, shapes, scratch, 10**9, 2 * 10**6, interpret)(other, *mine, weight, final)


def outer(place, both, pair, pair_mask, own_counts, other_counts, weight, interpret=False):
    scratch = [
        pltpu.VMEM((2 * SENT, ROWS, 128), F32),
        pltpu.VMEM((256, 128), F32),
        pltpu.VMEM((2048, 128), F32),
        pltpu.VMEM((256, 128), F32),
        pltpu.VMEM((CHIPS, 4, 256), BF16),
        pltpu.SemaphoreType.DMA,
    ]
    shapes = (jax.ShapeDtypeStruct((CHIPS, 4, 256), BF16), jax.ShapeDtypeStruct((64, 4, 128), BF16))
    kernel = functools.partial(outer_kernel, place)
    specs = (pl.BlockSpec(memory_space=pltpu.HBM), pl.BlockSpec(memory_space=pltpu.VMEM))
    return call(kernel, shapes, scratch, 10**9, 2 * 10**6, interpret, out_specs=specs)(
        both, pair, pair_mask, own_counts, other_counts, weight
    )


def my_place():
    return lax.axis_index("seq"), lax.axis_index("chip"), lax.axis_index("core")


def exchange(messages):
    return lax.all_to_all(messages, ("seq", "chip"), 0, 0, tiled=True)


def per_device(x, mask, resolved, pair, combined, bias_weight, final, sides, outer_weight):
    messages, resolved = pack(x, mask, pair, bias_weight, resolved)
    own = exchange(messages)
    other = lax.ppermute(own, "core", [(0, 1), (1, 0)])
    *mine, pair_mask, own_counts = first(my_place, own, combined, sides, resolved)
    messages, other_counts = attend(my_place, other, mine, combined, final)
    both = lax.all_gather(exchange(messages), "core", axis=0, tiled=True)
    return outer(my_place, both, pair, pair_mask, own_counts, other_counts, outer_weight)


def solution(mesh):
    crop, seq, res = (mesh.shape[a] for a in ("crop", "seq", "res"))
    fine = Mesh(mesh.devices.reshape(crop, seq, res // 2, 2), ("crop", "seq", "chip", "core"))
    rows, columns = ("crop", "seq"), ("chip", "core")
    placed = (P(rows, columns, None), P(rows, columns), P("crop"), P(rows, columns, None)) + (P(),) * 5
    return jax.shard_map(
        per_device,
        mesh=fine,
        in_specs=placed,
        out_specs=(P(rows, columns, None), P(rows, columns, None)),
        check_vma=False,
    )
```
